256 devices in a mesh: mp: 16 (over y, x_hi, core), seq: 8 (over z), dp: 2 (over x_lo).
Axes of the slice: x: 4 (x_hi: 2, x_lo: 2; x = x_hi * 2 + x_lo), y: 4, z: 8, core: 2. Of those that a mesh axis runs over, the one named last changes fastest.
Arguments:
- query_rows: bfloat16 [2, 1536, 2048], P('dp', 'seq'), may hold values from -6 to 6
- key_rows: bfloat16 [2, 1536, 2048], P('dp', 'seq'), may hold values from -6 to 6
- value_rows: bfloat16 [2, 1536, 2048], P('dp', 'seq'), may hold values from -6 to 6
- cotangent: bfloat16 [2, 1536, 2048], P('dp', 'seq'), may hold values from -0.15625 to 0.15625
- inner_rate: float32 [2, 1536], P('dp', 'seq'), may hold values from 0.00013950893 to 0.0013950893
- expand_master: float32 [2048, 8192], P(('seq', 'dp'), 'mp'), may hold values from -0.125 to 0.125
- reduce_master: float32 [8192, 2048], P('mp', ('seq', 'dp')), may hold values from -0.0625 to 0.0625
- expand_first: float32 [2048, 8192], P(('seq', 'dp'), 'mp'), may hold values from -1.25 to 1.25
- reduce_first: float32 [8192, 2048], P('mp', ('seq', 'dp')), may hold values from -1.25 to 1.25
- expand_second: float32 [2048, 8192], P(('seq', 'dp'), 'mp'), may hold values from 0.001 to 0.003
- reduce_second: float32 [8192, 2048], P('mp', ('seq', 'dp')), may hold values from 0.001 to 0.003
Outputs:
- mixed: bfloat16 [2, 1536, 2048], P('dp', 'seq', 'mp')
- expand_updated: float32 [2048, 8192], P(('seq', 'dp'), 'mp')
- reduce_updated: float32 [8192, 2048], P('mp', ('seq', 'dp'))
- expand_momentum: float32 [2048, 8192], P(('seq', 'dp'), 'mp')
- reduce_momentum: float32 [8192, 2048], P('mp', ('seq', 'dp'))
- expand_variance: float32 [2048, 8192], P(('seq', 'dp'), 'mp')
- reduce_variance: float32 [8192, 2048], P('mp', ('seq', 'dp'))
- expand_weights: bfloat16 [2048, 8192], P(None, 'mp')
- reduce_weights: bfloat16 [8192, 2048], P('mp')
The draws below stay inside these ranges and needn't reach their ends.
All inputs are finite; a program needn't handle non-finite values.
Results may differ from the reference program's by a relative error of at most 0.017.
Values may be sent and summed in bfloat16 or wider, within the bound.
A program may use at most 128 MiB of HBM per device.

```python
import math
import jax
import jax.numpy as jnp

D = 2048
H = 8192
STEP = 1000
BATCH = 2
LENGTH = 1536


def raised(values, rng, source, target, parts, factor):
    owner, partner = [(jnp.arange(values.shape[dim]) // (values.shape[dim] // parts)).reshape([-1 if axis == dim else 1 for axis in range(values.ndim)]) for dim in (source, target)]
    chosen = jax.random.permutation(rng, parts)[partner]
    strong = (owner == chosen) | (owner == (partner + parts // 2) % parts)
    return jnp.where(strong, factor * values, values)


def level_of(key, extent, pieces, smallest, top_value):
    loudness, own = 1.0, jax.random.fold_in(key, 6)
    for dim, parts in pieces:
        heights = jnp.exp(jax.random.uniform(jax.random.fold_in(own, dim), (parts,), jnp.float32, smallest / len(pieces), top_value / len(pieces)))
        loudness = loudness * jnp.repeat(heights, extent[dim] // parts).reshape([-1 if axis == dim else 1 for axis in range(len(extent))])
    return loudness


def bell_draw(key, extent, scale, most, cuts=(), held_as=jnp.bfloat16):
    drawn = scale * jax.random.normal(key, extent, jnp.float32)
    if cuts:
        drawn = drawn * level_of(key, extent, cuts, -0.22, 0.18)
    return jnp.clip(drawn, -most, most).astype(held_as)


def noise_with(key, dims, spread, limit, cuts, heavy, kind=jnp.bfloat16):
    entries = spread * jax.random.normal(key, dims, jnp.float32)
    if cuts:
        entries = entries * level_of(key, dims, cuts, -0.22, 0.18)
    return jnp.clip(raised(entries, jax.random.fold_in(key, 3), *heavy), -limit, limit).astype(kind)


def setup_inputs(seed: int = 0) -> dict:
    key_list = jax.random.split(jax.random.key(seed), 12)
    return {
        "query_rows": bell_draw(key_list[0], (BATCH, LENGTH, D), 1.0, 6.0, ((0, 2), (1, 8))),
        "key_rows": bell_draw(key_list[1], (BATCH, LENGTH, D), 1.0, 6.0, ((0, 2), (1, 8))),
        "value_rows": bell_draw(key_list[2], (BATCH, LENGTH, D), 1.0, 6.0, ((0, 2), (1, 8))),
        "cotangent": noise_with(key_list[3], (BATCH, LENGTH, D), 0.02, 0.15625, ((0, 2), (1, 8)), (1, 2, 8, 2.0)),
        "inner_rate": jnp.clip(jnp.exp(math.log(0.0013950893) - 2.3025851 * jax.random.uniform(key_list[4], (BATCH, LENGTH), jnp.float32) ** level_of(key_list[4], (BATCH, LENGTH), ((0, 2), (1, 8)), -0.2, 0.2)), 0.00013950893, 0.0013950893),
        "expand_master": bell_draw(key_list[5], (D, H), D ** -0.5, 0.125, ((0, 16), (1, 16)), jnp.float32),
        "reduce_master": bell_draw(key_list[6], (H, D), H ** -0.5, 0.0625, ((0, 16), (1, 16)), jnp.float32),
        "expand_first": bell_draw(key_list[7], (D, H), 0.2, 1.25, ((0, 16), (1, 16)), jnp.float32),
        "reduce_first": bell_draw(key_list[8], (H, D), 0.2, 1.25, ((0, 16), (1, 16)), jnp.float32),
        "expand_second": jnp.clip(jnp.exp(math.log(0.003) - 1.09861225 * jax.random.uniform(key_list[9], (D, H), jnp.float32) ** level_of(key_list[9], (D, H), ((0, 16), (1, 16)), -0.2, 0.2)), 0.001, 0.003),
        "reduce_second": jnp.clip(jnp.exp(math.log(0.003) - 1.09861225 * jax.random.uniform(key_list[10], (H, D), jnp.float32) ** level_of(key_list[10], (H, D), ((0, 16), (1, 16)), -0.2, 0.2)), 0.001, 0.003),
    }


gelu_scale = 0.7978845608028654
gelu_cubic = 0.044715
beta_first = 0.9
beta_second = 0.999
learn_rate = 0.001
weight_decay = 0.1
adam_eps = 1e-08

def gelu_value(value):
    return 0.5 * value * (1.0 + jnp.tanh(gelu_scale * (value + gelu_cubic * value * value * value)))

def gelu_slope(value):
    inner = jnp.tanh(gelu_scale * (value + gelu_cubic * value * value * value))
    return 0.5 * (1.0 + inner) + 0.5 * value * (1.0 - inner * inner) * gelu_scale * (1.0 + 3.0 * gelu_cubic * value * value)

def one_sequence(queries, keys, values, upstream, rates, expand_fast, reduce_fast):
    hidden = jnp.dot(keys, expand_fast, preferred_element_type=jnp.float32)
    act = gelu_value(hidden)
    act_b = act.astype(jnp.bfloat16)
    recon = jnp.dot(act_b, reduce_fast, preferred_element_type=jnp.float32)
    resid = keys.astype(jnp.float32) + recon - values.astype(jnp.float32)
    resid_b = resid.astype(jnp.bfloat16)
    d_hidden = jnp.dot(resid_b, reduce_fast.T, preferred_element_type=jnp.float32) * gelu_slope(hidden)
    dz_w = (rates[:, None] * d_hidden).astype(jnp.bfloat16)
    act_w = (rates[:, None] * act).astype(jnp.bfloat16)
    places = jnp.arange(queries.shape[0], dtype=jnp.int32)
    causal = places[:, None] >= places[None, :]
    first_score = jnp.where(causal, jnp.dot(queries, keys.T, preferred_element_type=jnp.float32), 0.0).astype(jnp.bfloat16)
    zq = jnp.dot(queries, expand_fast, preferred_element_type=jnp.float32) - jnp.dot(first_score, dz_w, preferred_element_type=jnp.float32)
    aq_b = gelu_value(zq).astype(jnp.bfloat16)
    second_score = jnp.where(causal, jnp.dot(aq_b, act_w.T, preferred_element_type=jnp.float32), 0.0).astype(jnp.bfloat16)
    mixed = queries.astype(jnp.float32) + jnp.dot(aq_b, reduce_fast, preferred_element_type=jnp.float32) - jnp.dot(second_score, resid_b, preferred_element_type=jnp.float32)
    reduce_grad = jnp.dot(aq_b.T, upstream, preferred_element_type=jnp.float32)
    third_score = jnp.where(causal, jnp.dot(upstream, resid_b.T, preferred_element_type=jnp.float32), 0.0).astype(jnp.bfloat16)
    d_act = jnp.dot(upstream, reduce_fast.T, preferred_element_type=jnp.float32) - jnp.dot(third_score, act_w, preferred_element_type=jnp.float32)
    dzq_b = (d_act * gelu_slope(zq)).astype(jnp.bfloat16)
    expand_grad = jnp.dot(queries.T, dzq_b, preferred_element_type=jnp.float32)
    return (mixed.astype(jnp.bfloat16), expand_grad, reduce_grad)

def adam_update(master, first, second, grad):
    momentum = beta_first * first + (1.0 - beta_first) * grad
    variance = beta_second * second + (1.0 - beta_second) * grad * grad
    first_corr = 1.0 - beta_first ** STEP
    second_corr = 1.0 - beta_second ** STEP
    updated = master - learn_rate * (momentum / first_corr / (jnp.sqrt(variance / second_corr) + adam_eps) + weight_decay * master)
    return (updated, momentum, variance)

def reference(query_rows, key_rows, value_rows, cotangent, inner_rate, expand_master, reduce_master, expand_first, reduce_first, expand_second, reduce_second):
    expand_fast = expand_master.astype(jnp.bfloat16)
    reduce_fast = reduce_master.astype(jnp.bfloat16)
    outputs = []
    expand_grad = jnp.zeros(expand_master.shape, jnp.float32)
    reduce_grad = jnp.zeros(reduce_master.shape, jnp.float32)
    for index in range(BATCH):
        mixed_one, expand_one, reduce_one = one_sequence(query_rows[index], key_rows[index], value_rows[index], cotangent[index], inner_rate[index], expand_fast, reduce_fast)
        outputs.append(mixed_one)
        expand_grad = expand_grad + expand_one
        reduce_grad = reduce_grad + reduce_one
    mixed = jnp.stack(outputs, axis=0)
    expand_updated, expand_momentum, expand_variance = adam_update(expand_master, expand_first, expand_second, expand_grad)
    reduce_updated, reduce_momentum, reduce_variance = adam_update(reduce_master, reduce_first, reduce_second, reduce_grad)
    return (mixed, expand_updated, reduce_updated, expand_momentum, reduce_momentum, expand_variance, reduce_variance, expand_updated.astype(jnp.bfloat16), reduce_updated.astype(jnp.bfloat16))
```

```python
import jax
import jax.numpy as jnp
from jax import lax
from jax.experimental import pallas as pl
from jax.experimental.pallas import tpu as pltpu
from jax.sharding import PartitionSpec as P

STEP = 1000
MESH = pl.DeviceIdType.MESH
F32 = jnp.float32
BF = jnp.bfloat16

gelu_scale = 0.7978845608028654
gelu_cubic = 0.044715
beta_first = 0.9
beta_second = 0.999
learn_rate = 0.001
weight_decay = 0.1
adam_eps = 1e-08

SEQ, DP, MP = 8, 2, 16
ROWS, D, HID = 192, 2048, 512
N_SEMS = 208


def gelu_both(value):
    inner = jnp.tanh(gelu_scale * (value + gelu_cubic * value * value * value))
    act = 0.5 * value * (1.0 + inner)
    slope = 0.5 * (1.0 + inner) + 0.5 * value * (1.0 - inner * inner) * gelu_scale * (
        1.0 + 3.0 * gelu_cubic * value * value
    )
    return act, slope


def adam_update(master, first, second, grad):
    momentum = beta_first * first + (1.0 - beta_first) * grad
    variance = beta_second * second + (1.0 - beta_second) * grad * grad
    first_corr = 1.0 - beta_first**STEP
    second_corr = 1.0 - beta_second**STEP
    updated = master - learn_rate * (
        momentum / first_corr / (jnp.sqrt(variance / second_corr) + adam_eps)
        + weight_decay * master
    )
    return (updated, momentum, variance)


def dot(a, b):
    return jnp.dot(a, b, preferred_element_type=F32)


def dot_nt(a, b):
    return lax.dot_general(a, b, (((1,), (1,)), ((), ())), preferred_element_type=F32)


def dot_tn(a, b):
    return lax.dot_general(a, b, (((0,), (0,)), ((), ())), preferred_element_type=F32)


def mod(a, n):
    return lax.rem(a + 2 * n, n)


class Wire:
    def __init__(self, send, recv):
        self.send, self.recv, self.count, self.sent = send, recv, 0, []

    def slot(self):
        self.count += 1
        assert self.count <= N_SEMS
        return self.count - 1

    def copy(self, src, dst, slot, to):
        return pltpu.make_async_remote_copy(
            src_ref=src,
            dst_ref=dst,
            send_sem=self.send.at[slot],
            recv_sem=self.recv.at[slot],
            device_id=to,
            device_id_type=MESH,
        )

    def start(self, src, dst, slot, to, cond=None):
        def go():
            self.copy(src, dst, slot, to).start()

        guarded(cond, go)
        self.sent.append((src, dst, slot, to, cond))

    def arrive(self, dst, slot, to, cond=None):
        def go():
            self.copy(dst, dst, slot, to).wait_recv()

        guarded(cond, go)

    def drain(self):
        for src, dst, slot, to, cond in self.sent:
            guarded(cond, lambda: self.copy(src, dst, slot, to).wait_send())
        self.sent = []


def guarded(cond, go):
    if cond is None:
        go()
    else:
        pl.when(cond)(go)


class Place:
    def __init__(self):
        self.m = lax.axis_index("mp")
        self.z = lax.axis_index("seq")
        self.d = lax.axis_index("dp")
        self.core = lax.rem(self.m, 2)
        self.chip = self.m // 2
        self.sibling = {"mp": self.chip * 2 + 1 - self.core}
        self.partner = {"dp": 1 - self.d}
        self.up = {"seq": mod(self.z + 1, SEQ)}
        self.down = {"seq": mod(self.z - 1, SEQ)}
        self.low = self.chip < 6

    def peer(self, off):
        return lax.rem(self.chip + off, 8)

    def source(self, off):
        return lax.rem(self.chip + 8 - off, 8)

    def chip_id(self, chip):
        return {"mp": chip * 2 + self.core}


class Ring:
    def __init__(self, w, p, view, cond=None, on_block=None, landing=None):
        self.w, self.p, self.view, self.cond, self.on_block = w, p, view, cond, on_block
        self.ups = [w.slot() for _ in range(4)]
        self.downs = [w.slot() for _ in range(3)]

    def go(self, block, up=None, down=None, src=None):
        ref = self.view(block)
        src = ref if src is None else src
        if up is not None:
            self.w.start(src, ref, self.ups[up], self.p.up, self.cond)
        if down is not None:
            self.w.start(src, ref, self.downs[down], self.p.down, self.cond)

    def start(self, src=None):
        self.go(self.p.z, 0, 0, src)

    def step(self, s):
        b = mod(self.p.z - s, SEQ)
        self.w.arrive(self.view(b), self.ups[s - 1], self.p.up, self.cond)
        if s < 4:
            self.go(b, up=s)
        if self.on_block:
            self.on_block(b, 2 * s - 1)
        if s < 4:
            b = mod(self.p.z + s, SEQ)
            self.w.arrive(self.view(b), self.downs[s - 1], self.p.down, self.cond)
            if s < 3:
                self.go(b, down=s)
            if self.on_block:
                self.on_block(b, 2 * s)


class Spread:
    def __init__(self, w, p, view, low):
        self.w, self.p, self.view, self.low = w, p, view, low
        self.far = [w.slot() for _ in range(8)]
        self.near = [w.slot() for _ in range(8)]

    def cond(self, chip):
        return chip < 6 if self.low else None

    def start(self):
        w, p = self.w, self.p
        own = self.view(p.m)
        for off in range(1, 8):
            w.start(own, own, self.far[off], p.chip_id(p.peer(off)), self.cond(p.chip))
        w.start(own, own, self.near[0], p.sibling, self.cond(p.chip))

    def relay(self):
        w, p = self.w, self.p
        for off in range(1, 8):
            src = p.source(off)
            ref = self.view(src * 2 + p.core)
            w.arrive(ref, self.far[off], p.chip_id(p.peer(off)), self.cond(src))
            w.start(ref, ref, self.near[off], p.sibling, self.cond(src))

    def finish(self):
        w, p = self.w, self.p
        for off in range(8):
            src = p.source(off)
            ref = self.view(src * 2 + 1 - p.core)
            w.arrive(ref, self.near[off], p.sibling, self.cond(src))


class Gather:
    def __init__(self, w, p, parts, near, far, low):
        self.w, self.p, self.parts, self.near, self.far, self.low = w, p, parts, near, far, low
        self.s_near = [w.slot() for _ in range(8)]
        self.s_far = [w.slot() for _ in range(8)]

    def cond(self, chip):
        return chip < 6 if self.low else None

    def compute(self, tile):
        w, p = self.w, self.p
        for off in (1, 2, 3, 4, 5, 6, 7, 0):
            chip = p.peer(off)

            def go():
                both = tile(chip)
                self.parts[0, chip] = both[:, :128].astype(BF)
                self.parts[1, chip] = both[:, 128:].astype(BF)

            guarded(self.cond(chip), go)
            w.start(
                self.parts.at[1 - p.core, chip],
                self.near.at[chip],
                self.s_near[off],
                p.sibling,
                self.cond(chip),
            )

    def relay(self):
        w, p = self.w, self.p
        for off in (1, 2, 3, 4, 5, 6, 7, 0):
            chip = p.peer(off)
            ref = self.near.at[chip]
            w.arrive(ref, self.s_near[off], p.sibling, self.cond(chip))

            def go():
                total = ref[...].astype(F32) + self.parts[p.core, chip].astype(F32)
                self.near[chip] = total.astype(BF)

            guarded(self.cond(chip), go)
            if off:
                w.start(ref, self.far.at[off], self.s_far[off], p.chip_id(chip), self.cond(chip))

    def finish(self):
        w, p = self.w, self.p
        total = self.near[p.chip].astype(F32)
        for off in range(1, 8):
            w.arrive(self.far.at[off], self.s_far[off], p.chip_id(p.peer(off)))
            total = total + self.far[off].astype(F32)
        return total


class Fold:
    def __init__(self, w, p, own, ups, downs):
        self.w, self.p, self.own, self.ups, self.downs = w, p, own, ups, downs
        self.s_up = [w.slot() for _ in range(4)]
        self.s_down = [w.slot() for _ in range(3)]

    def start(self, src_up, src_down):
        self.w.start(src_up, self.ups.at[0], self.s_up[0], self.p.up)
        self.w.start(src_down, self.downs.at[0], self.s_down[0], self.p.down)

    def step(self, s):
        w, p = self.w, self.p
        if s < 4:
            ref = self.ups.at[s - 1]
            w.arrive(ref, self.s_up[s - 1], p.up)
            ref[...] = (ref[...].astype(F32) + self.own(mod(p.z + 4 - s, SEQ))).astype(BF)
            w.start(ref, self.ups.at[s], self.s_up[s], p.up)
        if s < 3:
            ref = self.downs.at[s - 1]
            w.arrive(ref, self.s_down[s - 1], p.down)
            ref[...] = (ref[...].astype(F32) + self.own(mod(p.z - 3 + s, SEQ))).astype(BF)
            w.start(ref, self.downs.at[s], self.s_down[s], p.down)

    def finish(self):
        w, p = self.w, self.p
        w.arrive(self.downs.at[2], self.s_down[2], p.down)
        w.arrive(self.ups.at[3], self.s_up[3], p.up)
        return self.own(p.z) + self.ups[3].astype(F32) + self.downs[2].astype(F32)


def kernel(
    q_ref, k_ref, v_ref, c_ref, rate_ref,
    em_ref, rm_ref, e1_ref, r1_ref, e2_ref, r2_ref,
    mixed_ref, eu_ref, ru_ref, em1_ref, rm1_ref, ev_ref, rv_ref, ew_ref, rw_ref,
    ef, rf, k_rows, r_rows, act_all, dz_all, score1, score3, act_b, slope, resid, qe, cr,
    parts, near, far, parts2, near2, far2, parts3, near3, far3, own2, aq, dzq,
    g_r, x_r, up_r, down_r, g_e, x_e, up_e, down_e, w_e, w_r, send, recv, local,
):
    w, p = Wire(send, recv), Place()
    m, z, d = p.m, p.z, p.d

    barrier = pltpu.get_barrier_semaphore()
    friends = [p.up, p.down, p.partner, p.sibling]
    friends += [p.chip_id(p.peer(off)) for off in range(1, 8)]
    for friend in friends:
        pl.semaphore_signal(barrier, inc=1, device_id=friend, device_id_type=MESH)
    pl.semaphore_wait(barrier, len(friends))

    def e_block(j, dd):
        return pl.ds(pl.multiple_of(j * 256 + dd * 128, 128), 128)

    def e_pair(j):
        return pl.ds(pl.multiple_of(j * 256, 256), 256)

    def weights(full_e, full_r, own_e, own_r, extra):
        s_own, s_r = w.slot(), [w.slot() for _ in range(8)]
        mine = full_e.at[e_block(z, d), :]
        w.start(own_e, mine, s_own, p.partner)

        def forward(block, index, src=None):
            ref = full_r.at[:, e_block(block, d)]
            w.start(ref if src is None else src, ref, s_r[index], p.partner)

        ring_r = Ring(w, p, lambda j: full_r.at[:, e_block(j, d)], on_block=forward)
        ring_e = Ring(w, p, lambda j: full_e.at[e_pair(j), :])
        ring_r.start(own_r)
        forward(z, 0, own_r)
        w.arrive(full_e.at[e_block(z, 1 - d), :], s_own, p.partner)
        ring_e.start()
        for s in range(1, 5):
            extra(s)
            ring_e.step(s)
            ring_r.step(s)

        def finish():
            for index in range(8):
                hop = (index + 1) // 2
                block = mod(z - hop if index % 2 else z + hop, SEQ)
                w.arrive(full_r.at[:, e_block(block, 1 - d)], s_r[index], p.partner)

        return finish

    ef[e_block(z, d), :] = em_ref[...].astype(BF)
    rf[:, e_block(z, d)] = rm_ref[...].astype(BF)
    own_rows = pl.ds(pl.multiple_of(m * 16, 16), 16)

    def take_rows(out, rows_ref):
        def go():
            out[z] = rows_ref[own_rows, :]

        guarded(p.low, go)

    take_rows(k_rows, k_ref)
    ring_k = Ring(w, p, lambda j: k_rows.at[j], cond=p.low)
    ring_k.start()

    t_at = z * ROWS + lax.broadcasted_iota(jnp.int32, (ROWS, 128), 0)
    col = lax.broadcasted_iota(jnp.int32, (ROWS, 128), 1)
    s_at = (col // 16) * ROWS + m * 16 + lax.rem(col, 16)
    causal = t_at >= s_at

    def block_of(ref, block):
        return ref.at[:, pl.ds(pl.multiple_of(block * 128, 128), 128)]

    spread1 = Spread(w, p, lambda b: block_of(score1, b), True)
    spread_r = Spread(w, p, lambda b: block_of(resid, b), False)
    spread3 = Spread(w, p, lambda b: block_of(score3, b), True)

    def score(rows_ref, others, out):
        def go():
            part = dot_nt(rows_ref[...], others[...].reshape(128, D))
            block_of(out, m)[...] = jnp.where(causal, part, 0.0).astype(BF)

        guarded(p.low, go)

    def extra(s):
        ring_k.step(s)
        if s == 4:
            score(q_ref, k_rows, score1)
            spread1.start()

    mine_e, mine_r = ef.at[e_block(z, d), :], rf.at[:, e_block(z, d)]
    finish_weights = weights(ef, rf, mine_e, mine_r, extra)

    eye = lax.broadcasted_iota(jnp.int32, (ROWS, ROWS), 0) == lax.broadcasted_iota(
        jnp.int32, (ROWS, ROWS), 1
    )
    rates = jnp.sum(jnp.where(eye, rate_ref[...], 0.0), axis=1, keepdims=True)

    def put(ref, columns, value):
        ref[:, z, :, columns] = value.astype(BF).reshape(12, 16, 256)

    for n in range(2):
        columns = pl.ds(n * 256, 256)
        act, slope_n = gelu_both(dot(k_ref[...], ef[:, columns]))
        act_b[:, columns] = act.astype(BF)
        slope[:, columns] = slope_n
        put(act_all, columns, rates * act)
    ring_a = Ring(w, p, lambda j: act_all.at[:, j])
    ring_a.start()
    spread1.relay()
    finish_weights()

    sum1 = Gather(w, p, parts, near, far, False)

    def wide(chip):
        return pl.ds(pl.multiple_of(chip * 256, 256), 256)

    sum1.compute(lambda chip: dot(act_b[...], rf[:, wide(chip)]))
    sum1.relay()
    ring_a.step(1)
    recon = sum1.finish()
    block_of(resid, m)[...] = (
        block_of(k_ref, m)[...].astype(F32) + recon - block_of(v_ref, m)[...].astype(F32)
    ).astype(BF)
    spread_r.start()
    ring_a.step(2)
    for n in range(2):
        columns = pl.ds(n * 256, 256)
        qe[:, columns] = dot(q_ref[...], ef[:, columns])
        cr[:, columns] = dot_nt(c_ref[...], rf[columns, :])
    spread_r.relay()
    spread1.finish()
    spread_r.finish()

    take_rows(r_rows, resid)
    ring_rows = Ring(w, p, lambda j: r_rows.at[j], cond=p.low)
    ring_rows.start()
    for n in range(2):
        columns = pl.ds(n * 256, 256)
        d_hidden = dot_nt(resid[...], rf[columns, :]) * slope[:, columns]
        put(dz_all, columns, rates * d_hidden)
    ring_z = Ring(w, p, lambda j: dz_all.at[:, j])
    ring_z.start()
    ring_a.step(3)
    for s in range(1, 5):
        ring_rows.step(s)
        if s == 4:
            score(c_ref, r_rows, score3)
            spread3.start()
            ring_a.step(4)
        ring_z.step(s)

    for n in range(2):
        columns = pl.ds(n * 256, 256)
        zq = qe[:, columns] - dot(score1[...], dz_all[:, :, :, columns].reshape(1536, 256))
        act, slope_n = gelu_both(zq)
        aq[:, columns] = act.astype(BF)
        slope[:, columns] = slope_n

    order = (4, -3, 3, -2, 2, -1, 1, 0)
    s_x = [w.slot() for _ in range(8)]
    for i, off in enumerate(order):
        block = mod(z + off, SEQ)
        both = dot_tn(aq[...], c_ref[:, wide(block)])
        g_r[0, block] = both[:, :128].astype(BF)
        g_r[1, block] = both[:, 128:].astype(BF)
        w.start(g_r.at[1 - d, block], x_r.at[block], s_x[i], p.partner)
    spread3.relay()

    sum2 = Gather(w, p, parts2, near2, far2, True)
    sum2.compute(
        lambda chip: dot_nt(aq[...], act_all[pl.ds(2 * chip, 2)].reshape(256, HID))
    )
    spread3.finish()

    for n in range(2):
        columns = pl.ds(n * 256, 256)
        d_act = cr[:, columns] - dot(score3[...], act_all[:, :, :, columns].reshape(1536, 256))
        dzq[:, columns] = (d_act * slope[:, columns]).astype(BF)
    fold_e = Fold(w, p, lambda j: g_e[j].astype(F32), up_e, down_e)
    fold_r = Fold(w, p, lambda j: x_r[j].astype(F32), up_r, down_r)
    for i, off in enumerate(order):
        block = mod(z + off, SEQ)
        g_e[block] = dot_tn(q_ref[:, wide(block)], dzq[...]).astype(BF)
        if i == 1:
            fold_e.start(g_e.at[mod(z + 4, SEQ)], g_e.at[mod(z - 3, SEQ)])

    def take(i):
        block = mod(z + order[i], SEQ)
        ref = x_r.at[block]
        w.arrive(ref, s_x[i], p.partner)
        ref[...] = (ref[...].astype(F32) + g_r[d, block].astype(F32)).astype(BF)

    take(0)
    take(1)
    fold_r.start(x_r.at[mod(z + 4, SEQ)], x_r.at[mod(z - 3, SEQ)])
    sum2.relay()
    fold_e.step(1)
    take(2)
    take(3)
    fold_r.step(1)

    def own_score():
        own2[...] = jnp.where(causal, sum2.finish(), 0.0).astype(BF)

    pl.when(p.low)(own_score)
    sum3 = Gather(w, p, parts3, near3, far3, False)

    def mixed_tile(chip):
        first = dot(aq[...], rf[:, wide(chip)])
        return first - dot(own2[...], r_rows[:, :, wide(chip)].reshape(128, 256))

    pl.when(jnp.logical_not(p.low))(lambda: clear(own2, r_rows))
    sum3.compute(mixed_tile)
    fold_e.step(2)
    take(4)
    take(5)
    fold_r.step(2)
    sum3.relay()
    fold_e.step(3)
    take(6)
    fold_r.step(3)
    total = fold_e.finish()
    x_e[0] = total[:128].astype(BF)
    x_e[1] = total[128:].astype(BF)
    s_swap = w.slot()
    w.start(x_e.at[1 - d], x_e.at[2], s_swap, p.partner)
    mixed_ref[...] = (block_of(q_ref, m)[...].astype(F32) + sum3.finish()).astype(BF)
    take(7)

    w.arrive(x_e.at[2], s_swap, p.partner)
    grad = x_e[d].astype(F32) + x_e[2].astype(F32)
    eu, em1, ev = adam_update(em_ref[...], e1_ref[...], e2_ref[...], grad)
    eu_ref[...], em1_ref[...], ev_ref[...] = eu, em1, ev
    w_e[...] = eu.astype(BF)
    ru, rm1, rv = adam_update(rm_ref[...], r1_ref[...], r2_ref[...], fold_r.finish())
    ru_ref[...], rm1_ref[...], rv_ref[...] = ru, rm1, rv
    w_r[...] = ru.astype(BF)
    keep_e = pltpu.make_async_copy(w_e, ew_ref.at[e_block(z, d), :], local.at[0])
    keep_r = pltpu.make_async_copy(w_r, rw_ref.at[:, e_block(z, d)], local.at[1])
    keep_e.start()
    keep_r.start()
    keep_e.wait()
    keep_r.wait()
    finish_weights = weights(ew_ref, rw_ref, w_e, w_r, lambda s: None)
    finish_weights()
    w.drain()


def clear(*refs):
    for ref in refs:
        ref[...] = jnp.zeros(ref.shape, ref.dtype)


def body(
    query_rows, key_rows, value_rows, cotangent, inner_rate,
    expand_master, reduce_master, expand_first, reduce_first, expand_second, reduce_second,
):
    vmem = pl.BlockSpec(memory_space=pltpu.VMEM)
    hbm = pl.BlockSpec(memory_space=pl.ANY)
    e_shape, r_shape = expand_master.shape, reduce_master.shape

    def bf(*shape):
        return pltpu.VMEM(shape, BF)

    def f32(*shape):
        return pltpu.VMEM(shape, F32)

    outs = pl.pallas_call(
        kernel,
        out_shape=[
            jax.ShapeDtypeStruct((ROWS, 128), BF),
            jax.ShapeDtypeStruct(e_shape, F32),
            jax.ShapeDtypeStruct(r_shape, F32),
            jax.ShapeDtypeStruct(e_shape, F32),
            jax.ShapeDtypeStruct(r_shape, F32),
            jax.ShapeDtypeStruct(e_shape, F32),
            jax.ShapeDtypeStruct(r_shape, F32),
            jax.ShapeDtypeStruct((D, HID), BF),
            jax.ShapeDtypeStruct((HID, D), BF),
        ],
        in_specs=[vmem] * 11,
        out_specs=[vmem] * 7 + [hbm] * 2,
        scratch_shapes=[
            bf(D, HID), bf(HID, D),
            bf(SEQ, 16, D), bf(SEQ, 16, D),
            bf(12, SEQ, 16, HID), bf(12, SEQ, 16, HID),
            bf(ROWS, 1536), bf(ROWS, 1536),
            bf(ROWS, HID), f32(ROWS, HID),
            bf(ROWS, D), f32(ROWS, HID), f32(ROWS, HID),
            bf(2, 8, ROWS, 128), bf(8, ROWS, 128), bf(8, ROWS, 128),
            bf(2, 6, ROWS, 128), bf(6, ROWS, 128), bf(8, ROWS, 128),
            bf(2, 8, ROWS, 128), bf(8, ROWS, 128), bf(8, ROWS, 128),
            bf(ROWS, 128), bf(ROWS, HID), bf(ROWS, HID),
            bf(2, SEQ, HID, 128), bf(SEQ, HID, 128), bf(4, HID, 128), bf(3, HID, 128),
            bf(SEQ, 256, HID), bf(3, 128, HID), bf(4, 256, HID), bf(3, 256, HID),
            bf(128, HID), bf(HID, 128),
            pltpu.SemaphoreType.DMA((N_SEMS,)),
            pltpu.SemaphoreType.DMA((N_SEMS,)),
            pltpu.SemaphoreType.DMA((2,)),
        ],
        compiler_params=pltpu.CompilerParams(
            collective_id=0, has_side_effects=True, vmem_limit_bytes=56 * 1024 * 1024
        ),
        cost_estimate=pl.CostEstimate(
            flops=5_000_000_000, bytes_accessed=12_000_000, transcendentals=400_000
        ),
    )(
        query_rows[0], key_rows[0], value_rows[0], cotangent[0], inner_rate,
        expand_master, reduce_master, expand_first, reduce_first, expand_second, reduce_second,
    )
    return (outs[0][None], *outs[1:])


def solution(mesh):
    in_specs = (
        P("dp", "seq", None),
        P("dp", "seq", None),
        P("dp", "seq", None),
        P("dp", "seq", None),
        P("dp", "seq"),
        P(("seq", "dp"), "mp"),
        P("mp", ("seq", "dp")),
        P(("seq", "dp"), "mp"),
        P("mp", ("seq", "dp")),
        P(("seq", "dp"), "mp"),
        P("mp", ("seq", "dp")),
    )
    out_specs = (
        P("dp", "seq", "mp"),
        P(("seq", "dp"), "mp"),
        P("mp", ("seq", "dp")),
        P(("seq", "dp"), "mp"),
        P("mp", ("seq", "dp")),
        P(("seq", "dp"), "mp"),
        P("mp", ("seq", "dp")),
        P(None, "mp"),
        P("mp", None),
    )
    return jax.shard_map(body, mesh=mesh, in_specs=in_specs, out_specs=out_specs, check_vma=False)
```

```python
import jax
import jax.numpy as jnp
from jax import lax
from jax.experimental import pallas as pl
from jax.experimental.pallas import tpu as pltpu
from jax.sharding import PartitionSpec as P

STEP = 1000
MESH = pl.DeviceIdType.MESH
F32 = jnp.float32
BF = jnp.bfloat16

gelu_scale = 0.7978845608028654
gelu_cubic = 0.044715
beta_first = 0.9
beta_second = 0.999
learn_rate = 0.001
weight_decay = 0.1
adam_eps = 1e-08

SEQ, DP, MP = 8, 2, 16
ROWS, D, HID = 192, 2048, 512
N_SEMS = 288


def gelu_both(value):
    inner = jnp.tanh(gelu_scale * (value + gelu_cubic * value * value * value))
    act = 0.5 * value * (1.0 + inner)
    slope = 0.5 * (1.0 + inner) + 0.5 * value * (1.0 - inner * inner) * gelu_scale * (
        1.0 + 3.0 * gelu_cubic * value * value
    )
    return act, slope


def adam_update(master, first, second, grad):
    momentum = beta_first * first + (1.0 - beta_first) * grad
    variance = beta_second * second + (1.0 - beta_second) * grad * grad
    first_corr = 1.0 - beta_first**STEP
    second_corr = 1.0 - beta_second**STEP
    updated = master - learn_rate * (
        momentum / first_corr / (jnp.sqrt(variance / second_corr) + adam_eps)
        + weight_decay * master
    )
    return (updated, momentum, variance)


def dot(a, b):
    return jnp.dot(a, b, preferred_element_type=F32)


def dot_nt(a, b):
    return lax.dot_general(a, b, (((1,), (1,)), ((), ())), preferred_element_type=F32)


def dot_tn(a, b):
    return lax.dot_general(a, b, (((0,), (0,)), ((), ())), preferred_element_type=F32)


def mod(a, n):
    return lax.rem(a + 2 * n, n)


class Wire:
    def __init__(self, send, recv):
        self.send, self.recv, self.count, self.sent = send, recv, 0, []

    def slot(self, count=1):
        self.count += count
        assert self.count <= N_SEMS
        return self.count - count

    def copy(self, src, dst, slot, to):
        return pltpu.make_async_remote_copy(
            src_ref=src,
            dst_ref=dst,
            send_sem=self.send.at[slot],
            recv_sem=self.recv.at[slot],
            device_id=to,
            device_id_type=MESH,
        )

    def start(self, src, dst, slot, to, cond=None):
        def go():
            self.copy(src, dst, slot, to).start()

        guarded(cond, go)
        self.sent.append((src, dst, slot, to, cond))

    def arrive(self, dst, slot, to, cond=None):
        def go():
            self.copy(dst, dst, slot, to).wait_recv()

        guarded(cond, go)

    def drain(self):
        for src, dst, slot, to, cond in self.sent:
            guarded(cond, lambda: self.copy(src, dst, slot, to).wait_send())
        self.sent = []


def guarded(cond, go):
    if cond is None:
        go()
    else:
        pl.when(cond)(go)


class Place:
    def __init__(self):
        self.m = lax.axis_index("mp")
        self.z = lax.axis_index("seq")
        self.d = lax.axis_index("dp")
        self.core = lax.rem(self.m, 2)
        self.chip = self.m // 2
        self.sibling = {"mp": self.chip * 2 + 1 - self.core}
        self.partner = {"dp": 1 - self.d}
        self.up = {"seq": mod(self.z + 1, SEQ)}
        self.down = {"seq": mod(self.z - 1, SEQ)}
        self.low = self.chip < 6

    def peer(self, off):
        return lax.rem(self.chip + off, 8)

    def source(self, off):
        return lax.rem(self.chip + 8 - off, 8)

    def chip_id(self, chip):
        return {"mp": chip * 2 + self.core}


def span(base, half, size):
    if half is None:
        return pl.ds(base, size)
    return pl.ds(base + half * (size // 2), size // 2)


class Ring:
    def __init__(self, w, p, view, cond=None, on_block=None):
        self.w, self.p, self.view, self.cond, self.on_block = w, p, view, cond, on_block
        self.ups = [w.slot() for _ in range(4)]
        self.downs = [w.slot() for _ in range(4)]

    def start(self, src=None):
        ref = self.view(self.p.z, None)
        src = ref if src is None else src
        self.w.start(src, ref, self.ups[0], self.p.up, self.cond)
        self.w.start(src, ref, self.downs[0], self.p.down, self.cond)

    def hop(self, s, block, sems, to, half):
        now = half if s == 4 else None
        ref = self.view(block, now)
        self.w.arrive(ref, sems[s - 1], to, self.cond)
        if s < 4:
            later = self.view(block, half if s == 3 else None)
            self.w.start(later, later, sems[s], to, self.cond)
        if self.on_block:
            self.on_block(block, now, 2 * s - 1 + half)

    def step(self, s):
        z = self.p.z
        self.hop(s, mod(z - s, SEQ), self.ups, self.p.up, 0)
        self.hop(s, mod(z + s, SEQ), self.downs, self.p.down, 1)


class Share:
    def __init__(self, w, p, one_a, pair_a, one_b):
        self.w, self.p, self.one_a, self.one_b = w, p, one_a, one_b
        self.s_a = w.slot()
        self.s_b = [w.slot() for _ in range(9)]
        self.ring_a = Ring(w, p, pair_a)
        self.ring_b = Ring(
            w, p, lambda j, half: one_b(j, p.d, half), on_block=self.forward
        )

    def forward(self, block, half, index, src=None):
        ref = self.one_b(block, self.p.d, half)
        self.w.start(ref if src is None else src, ref, self.s_b[index], self.p.partner)

    def start_a(self, src):
        self.w.start(src, self.one_a(self.p.z, self.p.d), self.s_a, self.p.partner)

    def open_a(self):
        p = self.p
        self.w.arrive(self.one_a(p.z, 1 - p.d), self.s_a, p.partner)
        self.ring_a.start()

    def start_b(self, src):
        self.ring_b.start(src)
        self.forward(self.p.z, None, 0, src)

    def take_b(self, s):
        p = self.p
        if s == 0:
            self.w.arrive(self.one_b(p.z, 1 - p.d, None), self.s_b[0], p.partner)
            return
        for half, block in enumerate((mod(p.z - s, SEQ), mod(p.z + s, SEQ))):
            ref = self.one_b(block, 1 - p.d, half if s == 4 else None)
            self.w.arrive(ref, self.s_b[2 * s - 1 + half], p.partner)


class Spread:
    def __init__(self, w, p, view, low):
        self.w, self.p, self.view, self.low = w, p, view, low
        self.far = [w.slot() for _ in range(8)]
        self.near = [w.slot() for _ in range(8)]

    def cond(self, chip):
        return chip < 6 if self.low else None

    def start(self):
        w, p = self.w, self.p
        own = self.view(p.m)
        for off in range(1, 8):
            w.start(own, own, self.far[off], p.chip_id(p.peer(off)), self.cond(p.chip))
        w.start(own, own, self.near[0], p.sibling, self.cond(p.chip))

    def relay(self):
        w, p = self.w, self.p
        for off in range(1, 8):
            src = p.source(off)
            ref = self.view(src * 2 + p.core)
            w.arrive(ref, self.far[off], p.chip_id(p.peer(off)), self.cond(src))
            w.start(ref, ref, self.near[off], p.sibling, self.cond(src))

    def finish(self):
        w, p = self.w, self.p
        for off in range(8):
            src = p.source(off)
            ref = self.view(src * 2 + 1 - p.core)
            w.arrive(ref, self.near[off], p.sibling, self.cond(src))


class Gather:
    def __init__(self, w, p, parts, near, far, low):
        self.w, self.p, self.parts, self.near, self.far, self.low = w, p, parts, near, far, low
        self.s_near = w.slot(8)
        self.s_far = w.slot(8)

    def cond(self, chip):
        return chip < 6 if self.low else None

    def compute(self, chip, tile):
        def go():
            both = tile(chip)
            self.parts[0, chip] = both[:, :128].astype(BF)
            self.parts[1, chip] = both[:, 128:].astype(BF)

        guarded(self.cond(chip), go)
        self.w.start(
            self.parts.at[1 - self.p.core, chip],
            self.near.at[chip],
            self.s_near + chip,
            self.p.sibling,
            self.cond(chip),
        )

    def compute_all(self, tile):
        for off in (1, 2, 3, 4, 5, 6, 7, 0):
            self.compute(self.p.peer(off), tile)

    def relay(self):
        w, p = self.w, self.p
        for off in (1, 2, 3, 4, 5, 6, 7, 0):
            chip = p.peer(off)
            ref = self.near.at[chip]
            w.arrive(ref, self.s_near + chip, p.sibling, self.cond(chip))

            def go():
                total = ref[...].astype(F32) + self.parts[p.core, chip].astype(F32)
                self.near[chip] = total.astype(BF)

            guarded(self.cond(chip), go)
            if off:
                to = p.chip_id(chip)
                w.start(ref, self.far.at[off], self.s_far + off, to, self.cond(chip))

    def finish(self):
        w, p = self.w, self.p
        total = self.near[p.chip].astype(F32)
        for off in range(1, 8):
            w.arrive(self.far.at[off], self.s_far + off, p.chip_id(p.peer(off)))
            total = total + self.far[off].astype(F32)
        return total


class Fold:
    def __init__(self, w, p, own, up_half, down_half, ups, downs):
        self.w, self.p, self.own = w, p, own
        self.halves = (up_half, down_half)
        self.full = (ups, downs)
        self.sems = ([w.slot() for _ in range(4)], [w.slot() for _ in range(4)])

    def way(self, side):
        return self.p.down if side else self.p.up

    def start(self):
        for side in range(2):
            src = self.own(mod(self.p.z + 4, SEQ), side)
            self.w.start(src, self.halves[side], self.sems[side][0], self.way(side))

    def step(self, s):
        w = self.w
        for side in range(2):
            away = s - 4 if side else 4 - s
            block = mod(self.p.z + away, SEQ)
            out = self.full[side].at[s - 1]
            if s == 1:
                got, held = self.halves[side], self.own(block, side)
                w.arrive(got, self.sems[side][0], self.way(side))
                held[...] = (held[...].astype(F32) + got[...].astype(F32)).astype(BF)
                ref = self.own(block, None)
            else:
                ref, term = self.full[side].at[s - 2], self.own(block, None)
                w.arrive(ref, self.sems[side][s - 1], self.way(side))
                ref[...] = (ref[...].astype(F32) + term[...].astype(F32)).astype(BF)
            w.start(ref, out, self.sems[side][s], self.way(side))

    def finish(self):
        total = self.own(self.p.z, None)[...].astype(F32)
        for side in range(2):
            ref = self.full[side].at[2]
            self.w.arrive(ref, self.sems[side][3], self.way(side))
            total = total + ref[...].astype(F32)
        return total


def take_turns(*tasks):
    tasks = list(tasks)
    while tasks:
        for task in list(tasks):
            if next(task, "done") == "done":
                tasks.remove(task)


ORDER = (4, 3, -3, 2, -2, 1, -1, 0)


def kernel(
    q_in, k_in, v_in, c_in, rate_in,
    em_in, rm_in, e1_in, r1_in, e2_in, r2_in,
    mixed_ref, eu_ref, ru_ref, em1_ref, rm1_ref, ev_ref, rv_ref, ew_ref, rw_ref,
    q_ref, k_ref, v_ref, c_ref, rate_ref, em_ref, rm_ref, e1_ref, r1_ref, e2_ref, r2_ref,
    ef, rf, k_rows, r_rows, act_all, dz_all, score1, score3, act_b, slope, resid, qe, cr,
    parts, near, far, parts2, near2, far2, parts3, near3, far3, own2, aq, dzq,
    ga_e, gb_e, xb_e, ga_r, gb_r, xb_r, ha, hb_e, hb_r, fa, fb_e, fb_r, swap_e, swap_r,
    w_e, w_r, send, recv, local,
):
    w, p = Wire(send, recv), Place()
    m, z, d = p.m, p.z, p.d

    loads = {}
    for index, (src, dst) in enumerate(
        (
            (em_in, em_ref), (rm_in, rm_ref), (k_in, k_ref), (rate_in, rate_ref),
            (v_in, v_ref), (q_in, q_ref), (c_in, c_ref), (e1_in, e1_ref), (r1_in, r1_ref),
            (e2_in, e2_ref), (r2_in, r2_ref),
        )
    ):
        loads[index] = pltpu.make_async_copy(src, dst, local.at[index])
        loads[index].start()

    barrier = pltpu.get_barrier_semaphore()
    friends = [p.up, p.down, p.partner, p.sibling]
    friends += [p.chip_id(p.peer(off)) for off in range(1, 8)]
    for friend in friends:
        pl.semaphore_signal(barrier, inc=1, device_id=friend, device_id_type=MESH)
    pl.semaphore_wait(barrier, len(friends))

    def block_at(j, dd):
        return pl.multiple_of(j * 256 + dd * 128, 128)

    def pair_at(j):
        return pl.multiple_of(j * 256, 256)

    def share_e(full):
        return Share(
            w,
            p,
            lambda j, dd: full.at[pl.ds(block_at(j, dd), 128), 0:256],
            lambda j, half: full.at[span(pair_at(j), half, 256), 0:256],
            lambda j, dd, half: full.at[span(block_at(j, dd), half, 128), 256:512],
        )

    def share_r(full):
        return Share(
            w,
            p,
            lambda j, dd: full.at[0:256, pl.ds(block_at(j, dd), 128)],
            lambda j, half: full.at[span(0, half, 256), pl.ds(pair_at(j), 256)],
            lambda j, dd, half: full.at[span(256, half, 256), pl.ds(block_at(j, dd), 128)],
        )

    share1, share2 = share_e(ef), share_r(rf)
    loads[0].wait()
    ef[pl.ds(block_at(z, d), 128), :] = em_ref[...].astype(BF)
    share1.start_a(share1.one_a(z, d))
    share1.start_b(share1.one_b(z, d, None))
    loads[1].wait()
    rf[:, pl.ds(block_at(z, d), 128)] = rm_ref[...].astype(BF)
    share1.open_a()
    share2.start_a(share2.one_a(z, d))
    for index in (2, 3, 4, 5, 6):
        loads[index].wait()

    t_at = z * ROWS + lax.broadcasted_iota(jnp.int32, (ROWS, 128), 0)
    col = lax.broadcasted_iota(jnp.int32, (ROWS, 128), 1)
    s_at = (col // 16) * ROWS + m * 16 + lax.rem(col, 16)
    causal = t_at >= s_at
    eye = lax.broadcasted_iota(jnp.int32, (ROWS, ROWS), 0) == lax.broadcasted_iota(
        jnp.int32, (ROWS, ROWS), 1
    )
    rates = jnp.sum(jnp.where(eye, rate_ref[...], 0.0), axis=1, keepdims=True)

    own_rows = pl.ds(pl.multiple_of(m * 16, 16), 16)

    def take_rows(out, rows_ref):
        def go():
            out[z] = rows_ref[own_rows, :]

        guarded(p.low, go)

    def block_of(ref, block):
        return ref.at[:, pl.ds(pl.multiple_of(block * 128, 128), 128)]

    def wide(chip):
        return pl.ds(pl.multiple_of(chip * 256, 256), 256)

    spread1 = Spread(w, p, lambda b: block_of(score1, b), True)
    spread_r = Spread(w, p, lambda b: block_of(resid, b), False)
    spread3 = Spread(w, p, lambda b: block_of(score3, b), True)

    def score(rows_ref, others, out):
        def go():
            part = dot_nt(rows_ref[...], others[...].reshape(128, D))
            block_of(out, m)[...] = jnp.where(causal, part, 0.0).astype(BF)

        guarded(p.low, go)

    def put(ref, columns, value):
        ref[:, z, :, columns] = value.astype(BF).reshape(12, 16, 256)

    def rows_ring(ref):
        return Ring(w, p, lambda j, half: ref.at[j, :, span(0, half, D)], cond=p.low)

    def hidden_ring(ref):
        return Ring(w, p, lambda j, half: ref.at[span(0, half, 12), j])

    take_rows(k_rows, k_ref)
    ring_k, ring_rows = rows_ring(k_rows), rows_ring(r_rows)
    ring_a, ring_z = hidden_ring(act_all), hidden_ring(dz_all)

    def step1(s):
        share1.ring_a.step(s)
        share1.ring_b.step(s)

    def step2(s):
        share2.ring_a.step(s)
        share2.ring_b.step(s)

    step1(1)
    share2.start_b(share2.one_b(z, d, None))
    step1(2)
    share2.open_a()
    step1(3)
    step1(4)
    step2(1)
    for s in range(5):
        share1.take_b(s)

    for n in range(2):
        columns = pl.ds(n * 256, 256)
        act, slope_n = gelu_both(dot(k_ref[...], ef[:, columns]))
        act_b[:, columns] = act.astype(BF)
        slope[:, columns] = slope_n
        put(act_all, columns, rates * act)

    sum1 = Gather(w, p, parts, near, far, False)

    def recon_tile(chip):
        return dot(act_b[...], rf[:, wide(chip)])

    step2(2)
    share2.take_b(0)
    sum1.compute(z, recon_tile)
    step2(3)
    ring_a.start()
    ring_k.start()
    for s in (1, 2, 3):
        share2.take_b(s)
        sum1.compute(mod(z - s, SEQ), recon_tile)
        sum1.compute(mod(z + s, SEQ), recon_tile)
    step2(4)
    share2.take_b(4)
    sum1.compute(mod(z + 4, SEQ), recon_tile)
    sum1.relay()
    ring_a.step(1)
    ring_k.step(1)
    for n in range(2):
        columns = pl.ds(n * 256, 256)
        qe[:, columns] = dot(q_ref[...], ef[:, columns])
    recon = sum1.finish()
    block_of(resid, m)[...] = (
        block_of(k_ref, m)[...].astype(F32) + recon - block_of(v_ref, m)[...].astype(F32)
    ).astype(BF)
    spread_r.start()
    ring_a.step(2)
    ring_k.step(2)
    for n in range(2):
        columns = pl.ds(n * 256, 256)
        cr[:, columns] = dot_nt(c_ref[...], rf[columns, :])
    spread_r.relay()
    ring_a.step(3)
    ring_k.step(3)
    spread_r.finish()

    for n in range(2):
        columns = pl.ds(n * 256, 256)
        d_hidden = dot_nt(resid[...], rf[columns, :]) * slope[:, columns]
        put(dz_all, columns, rates * d_hidden)
    ring_z.start()
    take_rows(r_rows, resid)
    ring_rows.start()
    ring_a.step(4)
    ring_k.step(4)
    score(q_ref, k_rows, score1)
    spread1.start()
    ring_z.step(1)
    ring_rows.step(1)
    spread1.relay()
    ring_z.step(2)
    ring_rows.step(2)
    spread1.finish()
    ring_z.step(3)
    ring_rows.step(3)
    ring_z.step(4)

    for n in range(2):
        columns = pl.ds(n * 256, 256)
        zq = qe[:, columns] - dot(score1[...], dz_all[:, :, :, columns].reshape(1536, 256))
        act, slope_n = gelu_both(zq)
        aq[:, columns] = act.astype(BF)
        slope[:, columns] = slope_n

    s_xe, s_xr = [w.slot() for _ in range(8)], [w.slot() for _ in range(8)]
    fold_ar = Fold(
        w, p, lambda j, half: ga_r.at[j, span(0, half, 256)],
        ha.at[0], ha.at[1], fa.at[0], fa.at[1],
    )
    fold_ae = Fold(
        w, p, lambda j, half: ga_e.at[j, span(0, half, 256)],
        ha.at[2], ha.at[3], fa.at[2], fa.at[3],
    )
    fold_br = Fold(
        w, p, lambda j, half: xb_r.at[j, span(0, half, 256)],
        hb_r.at[0], hb_r.at[1], fb_r.at[0], fb_r.at[1],
    )
    fold_be = Fold(
        w, p, lambda j, half: xb_e.at[j, span(0, half, 128)],
        hb_e.at[0], hb_e.at[1], fb_e.at[0], fb_e.at[1],
    )
    for i, off in enumerate(ORDER):
        block = mod(z + off, SEQ)
        both = dot_tn(aq[...], c_ref[:, wide(block)])
        ga_r[block] = both[:256].astype(BF)
        gb_r[0, block] = both[256:, :128].astype(BF)
        gb_r[1, block] = both[256:, 128:].astype(BF)
        w.start(gb_r.at[1 - d, block], xb_r.at[block], s_xr[i], p.partner)
        if i == 0:
            fold_ar.start()
    ring_rows.step(4)
    score(c_ref, r_rows, score3)
    spread3.start()

    sum2 = Gather(w, p, parts2, near2, far2, True)
    sum2.compute_all(
        lambda chip: dot_nt(aq[...], act_all[pl.ds(2 * chip, 2)].reshape(256, HID))
    )
    spread3.relay()
    sum2.relay()
    fold_ar.step(1)
    spread3.finish()

    for n in range(2):
        columns = pl.ds(n * 256, 256)
        d_act = cr[:, columns] - dot(score3[...], act_all[:, :, :, columns].reshape(1536, 256))
        dzq[:, columns] = (d_act * slope[:, columns]).astype(BF)
    for i, off in enumerate(ORDER):
        block = mod(z + off, SEQ)
        both = dot_tn(q_ref[:, wide(block)], dzq[...])
        ga_e[block] = both[:, :256].astype(BF)
        gb_e[0, block] = both[:128, 256:].astype(BF)
        gb_e[1, block] = both[128:, 256:].astype(BF)
        w.start(gb_e.at[1 - d, block], xb_e.at[block], s_xe[i], p.partner)
        if i == 0:
            fold_ae.start()

    for index in (7, 8, 9, 10):
        loads[index].wait()
    share3, share4 = share_e(ew_ref), share_r(rw_ref)
    keeps = []

    def optimizer(is_e, part, grad):
        refs = (
            (em_ref, e1_ref, e2_ref, eu_ref, em1_ref, ev_ref, w_e)
            if is_e
            else (rm_ref, r1_ref, r2_ref, ru_ref, rm1_ref, rv_ref, w_r)
        )
        at = pl.ds(256 * part, 256)
        at = (slice(None), at) if is_e else (at, slice(None))
        outs = adam_update(refs[0][at], refs[1][at], refs[2][at], grad)
        refs[3][at], refs[4][at], refs[5][at] = outs
        refs[6][at] = outs[0].astype(BF)
        own = refs[6].at[at]
        share = share3 if is_e else share4
        home = share.one_b(z, d, None) if part else share.one_a(z, d)
        keep = pltpu.make_async_copy(own, home, local.at[11 + len(keeps)])
        keep.start()
        keeps.append(keep)
        return share, own, keep

    def part_a(is_e, fold, swap, first):
        for s in range(first, 4):
            fold.step(s)
            yield
        total = fold.finish()
        for dd in range(2):
            at = pl.ds(dd * 128, 128)
            swap[dd] = (total[128 * dd : 128 * dd + 128] if is_e else total[:, 128 * dd : 128 * dd + 128]).astype(BF)
        slot = w.slot()
        w.start(swap.at[1 - d], swap.at[2], slot, p.partner)
        yield
        w.arrive(swap.at[2], slot, p.partner)
        grad = swap[d].astype(F32) + swap[2].astype(F32)
        share, own, keep = optimizer(is_e, 0, grad)
        share.start_a(own)
        yield
        keep.wait()
        share.open_a()
        for s in range(1, 5):
            yield
            share.ring_a.step(s)

    def part_b(is_e, fold, mine, got, sems):
        def take(i):
            block = mod(z + ORDER[i], SEQ)
            ref = got.at[block]
            w.arrive(ref, sems[i], p.partner)
            ref[...] = (ref[...].astype(F32) + mine[d, block].astype(F32)).astype(BF)

        take(0)
        fold.start()
        yield
        for s in range(1, 4):
            take(2 * s - 1)
            take(2 * s)
            fold.step(s)
            yield
        take(7)
        share, own, keep = optimizer(is_e, 1, fold.finish())
        share.start_b(own)
        for s in range(1, 5):
            yield
            share.ring_b.step(s)
        for s in range(5):
            yield
            share.take_b(s)
        keep.wait()

    def output():
        pl.when(p.low)(own_score)
        pl.when(jnp.logical_not(p.low))(lambda: clear(own2, r_rows))
        sum3 = Gather(w, p, parts3, near3, far3, False)
        sum3.compute_all(mixed_tile)
        yield
        sum3.relay()
        yield
        mixed_ref[...] = (block_of(q_ref, m)[...].astype(F32) + sum3.finish()).astype(BF)

    def own_score():
        own2[...] = jnp.where(causal, sum2.finish(), 0.0).astype(BF)

    def mixed_tile(chip):
        first = dot(aq[...], rf[:, wide(chip)])
        return first - dot(own2[...], r_rows[:, :, wide(chip)].reshape(128, 256))

    take_turns(
        part_b(False, fold_br, gb_r, xb_r, s_xr),
        part_a(False, fold_ar, swap_r, 2),
        part_a(True, fold_ae, swap_e, 1),
        part_b(True, fold_be, gb_e, xb_e, s_xe),
        output(),
    )
    w.drain()


def clear(*refs):
    for ref in refs:
        ref[...] = jnp.zeros(ref.shape, ref.dtype)


def pass_on(*refs):
    *arrays, sems = refs
    count = len(arrays) // 3
    ins, outs = [], []
    for src, dst, held in zip(arrays[:count], arrays[count : 2 * count], arrays[2 * count :]):
        pieces = 4 if src.shape[0] * src.shape[1] > 100_000 else 1
        size = src.shape[0] // pieces
        for piece in range(pieces):
            rows = pl.ds(piece * size, size)
            index = len(ins)
            ins.append(pltpu.make_async_copy(src.at[rows], held.at[rows], sems.at[0, index]))
            outs.append(pltpu.make_async_copy(held.at[rows], dst.at[rows], sems.at[1, index]))
            ins[-1].start()
    for copy_in, copy_out in zip(ins, outs):
        copy_in.wait()
        copy_out.start()
    for copy_out in outs:
        copy_out.wait()


def body(
    query_rows, key_rows, value_rows, cotangent, inner_rate,
    expand_master, reduce_master, expand_first, reduce_first, expand_second, reduce_second,
):
    vmem = pl.BlockSpec(memory_space=pltpu.VMEM)
    hbm = pl.BlockSpec(memory_space=pl.ANY)
    e_shape, r_shape = expand_master.shape, reduce_master.shape

    def bf(*shape):
        return pltpu.VMEM(shape, BF)

    def f32(*shape):
        return pltpu.VMEM(shape, F32)

    outs = pl.pallas_call(
        kernel,
        out_shape=[
            jax.ShapeDtypeStruct((ROWS, 128), BF),
            jax.ShapeDtypeStruct(e_shape, F32),
            jax.ShapeDtypeStruct(r_shape, F32),
            jax.ShapeDtypeStruct(e_shape, F32),
            jax.ShapeDtypeStruct(r_shape, F32),
            jax.ShapeDtypeStruct(e_shape, F32),
            jax.ShapeDtypeStruct(r_shape, F32),
            jax.ShapeDtypeStruct((D, HID), BF),
            jax.ShapeDtypeStruct((HID, D), BF),
        ],
        in_specs=[hbm] * 11,
        out_specs=[vmem] * 7 + [hbm] * 2,
        scratch_shapes=[
            bf(ROWS, D), bf(ROWS, D), bf(ROWS, D), bf(ROWS, D), f32(1, ROWS),
            f32(*e_shape), f32(*r_shape), f32(*e_shape), f32(*r_shape), f32(*e_shape), f32(*r_shape),
            bf(D, HID), bf(HID, D),
            bf(SEQ, 16, D), bf(SEQ, 16, D),
            bf(12, SEQ, 16, HID), bf(12, SEQ, 16, HID),
            bf(ROWS, 1536), bf(ROWS, 1536),
            bf(ROWS, HID), f32(ROWS, HID),
            bf(ROWS, D), f32(ROWS, HID), f32(ROWS, HID),
            bf(2, 8, ROWS, 128), bf(8, ROWS, 128), bf(8, ROWS, 128),
            bf(2, 6, ROWS, 128), bf(6, ROWS, 128), bf(8, ROWS, 128),
            bf(2, 8, ROWS, 128), bf(8, ROWS, 128), bf(8, ROWS, 128),
            bf(ROWS, 128), bf(ROWS, HID), bf(ROWS, HID),
            bf(SEQ, 256, 256), bf(2, SEQ, 128, 256), bf(SEQ, 128, 256),
            bf(SEQ, 256, 256), bf(2, SEQ, 256, 128), bf(SEQ, 256, 128),
            bf(4, 128, 256), bf(2, 64, 256), bf(2, 128, 128),
            bf(4, 3, 256, 256), bf(2, 3, 128, 256), bf(2, 3, 256, 128),
            bf(3, 128, 256), bf(3, 256, 128),
            bf(128, HID), bf(HID, 128),
            pltpu.SemaphoreType.DMA((N_SEMS,)),
            pltpu.SemaphoreType.DMA((N_SEMS,)),
            pltpu.SemaphoreType.DMA((16,)),
        ],
        compiler_params=pltpu.CompilerParams(
            collective_id=0, has_side_effects=True, vmem_limit_bytes=56 * 1024 * 1024
        ),
        cost_estimate=pl.CostEstimate(
            flops=5_000_000_000, bytes_accessed=12_000_000, transcendentals=400_000
        ),
    )(
        query_rows[0], key_rows[0], value_rows[0], cotangent[0], inner_rate,
        expand_master, reduce_master, expand_first, reduce_first, expand_second, reduce_second,
    )
    outs = pl.pallas_call(
        pass_on,
        out_shape=[jax.ShapeDtypeStruct(out.shape, out.dtype) for out in outs],
        in_specs=[hbm] * 9,
        out_specs=[hbm] * 9,
        scratch_shapes=[pltpu.VMEM(out.shape, out.dtype) for out in outs]
        + [pltpu.SemaphoreType.DMA((2, 16))],
        compiler_params=pltpu.CompilerParams(vmem_limit_bytes=60 * 1024 * 1024),
        cost_estimate=pl.CostEstimate(flops=0, bytes_accessed=12_000_000, transcendentals=0),
    )(*outs)
    return (outs[0][None], *outs[1:])


def solution(mesh):
    in_specs = (
        P("dp", "seq", None),
        P("dp", "seq", None),
        P("dp", "seq", None),
        P("dp", "seq", None),
        P("dp", "seq"),
        P(("seq", "dp"), "mp"),
        P("mp", ("seq", "dp")),
        P(("seq", "dp"), "mp"),
        P("mp", ("seq", "dp")),
        P(("seq", "dp"), "mp"),
        P("mp", ("seq", "dp")),
    )
    out_specs = (
        P("dp", "seq", "mp"),
        P(("seq", "dp"), "mp"),
        P("mp", ("seq", "dp")),
        P(("seq", "dp"), "mp"),
        P("mp", ("seq", "dp")),
        P(("seq", "dp"), "mp"),
        P("mp", ("seq", "dp")),
        P(None, "mp"),
        P("mp", None),
    )
    return jax.shard_map(body, mesh=mesh, in_specs=in_specs, out_specs=out_specs, check_vma=False)
```

```python
import jax
import jax.numpy as jnp
from jax import lax
from jax.experimental import pallas as pl
from jax.experimental.pallas import tpu as pltpu
from jax.sharding import PartitionSpec as P

STEP = 1000
MESH = pl.DeviceIdType.MESH
F32 = jnp.float32
BF = jnp.bfloat16

gelu_scale = 0.7978845608028654
gelu_cubic = 0.044715
beta_first = 0.9
beta_second = 0.999
learn_rate = 0.001
weight_decay = 0.1
adam_eps = 1e-08

SEQ, DP, MP = 8, 2, 16
ROWS, D, HID = 192, 2048, 512
N_RECV, N_SEND = 424, 64


def gelu_both(value):
    inner = jnp.tanh(gelu_scale * (value + gelu_cubic * value * value * value))
    act = 0.5 * value * (1.0 + inner)
    slope = 0.5 * (1.0 + inner) + 0.5 * value * (1.0 - inner * inner) * gelu_scale * (
        1.0 + 3.0 * gelu_cubic * value * value
    )
    return act, slope


def adam_update(master, first, second, grad):
    momentum = beta_first * first + (1.0 - beta_first) * grad
    variance = beta_second * second + (1.0 - beta_second) * grad * grad
    first_corr = 1.0 - beta_first**STEP
    second_corr = 1.0 - beta_second**STEP
    updated = master - learn_rate * (
        momentum / first_corr / (jnp.sqrt(variance / second_corr) + adam_eps)
        + weight_decay * master
    )
    return (updated, momentum, variance)


def dot(a, b):
    return jnp.dot(a, b, preferred_element_type=F32)


def dot_nt(a, b):
    return lax.dot_general(a, b, (((1,), (1,)), ((), ())), preferred_element_type=F32)


def dot_tn(a, b):
    return lax.dot_general(a, b, (((0,), (0,)), ((), ())), preferred_element_type=F32)


def mod(a, n):
    return lax.rem(a + 2 * n, n)


class Batch:
    def __init__(self, w, cond=None, counts=None):
        self.sem, self.rows, self.cond, self.counts = len(w.batches), 0, cond, counts
        w.batches.append(self)
        assert self.sem < N_SEND


class Wire:
    def __init__(self, send, recv, dummy):
        self.send, self.recv, self.dummy = send, recv, dummy
        self.count, self.batches = 0, []

    def slot(self, count=1):
        self.count += count
        assert self.count <= N_RECV
        return self.count - count

    def copy(self, src, dst, slot, to, out=0):
        return pltpu.make_async_remote_copy(
            src_ref=src,
            dst_ref=dst,
            send_sem=self.send.at[out],
            recv_sem=self.recv.at[slot],
            device_id=to,
            device_id_type=MESH,
        )

    def start(self, src, dst, slot, to, batch, cond=None):
        guarded(cond, lambda: self.copy(src, dst, slot, to, batch.sem).start())
        size = 1
        for extent in src.shape:
            size *= extent
        batch.rows += size // HID

    def arrive(self, dst, slot, to, cond=None):
        guarded(cond, lambda: self.copy(dst, dst, slot, to).wait_recv())

    def wait(self, sem, rows):
        ref = self.dummy.at[0:rows]
        pltpu.make_async_copy(ref, ref, sem).wait()

    def drain(self):
        for batch in self.batches:
            if not batch.rows:
                continue
            for cond, rows in batch.counts or ((batch.cond, batch.rows),):
                guarded(cond, lambda: self.wait(self.send.at[batch.sem], rows))


def guarded(cond, go):
    if cond is None:
        go()
    else:
        pl.when(cond)(go)


class Place:
    def __init__(self):
        self.m = lax.axis_index("mp")
        self.z = lax.axis_index("seq")
        self.d = lax.axis_index("dp")
        self.core = lax.rem(self.m, 2)
        self.chip = self.m // 2
        self.sibling = {"mp": self.chip * 2 + 1 - self.core}
        self.partner = {"dp": 1 - self.d}
        self.up = {"seq": mod(self.z + 1, SEQ)}
        self.down = {"seq": mod(self.z - 1, SEQ)}
        self.up2 = {"seq": mod(self.z + 2, SEQ)}
        self.down2 = {"seq": mod(self.z - 2, SEQ)}
        self.low = self.chip < 6

    def peer(self, off):
        return lax.rem(self.chip + off, 8)

    def source(self, off):
        return lax.rem(self.chip + 8 - off, 8)

    def others(self, rows):
        return ((self.low, 5 * rows), (jnp.logical_not(self.low), 6 * rows))

    def chip_id(self, chip):
        return {"mp": chip * 2 + self.core}


def span(base, part, size):
    if part is None:
        return pl.ds(base, size)
    i, n = part
    return pl.ds(base + i * (size // n), size // n)


class Ring:
    def __init__(self, w, p, view, chunks=1, cond=None, on_chunk=None):
        self.w, self.p, self.view, self.chunks = w, p, view, chunks
        self.cond, self.on_chunk, self.batch = cond, on_chunk, Batch(w, cond)
        self.sems = [[w.slot(4) for _ in range(chunks)] for _ in range(2)]
        self.to = (p.up, p.down)

    def part(self, c, half=None):
        return (c, self.chunks) if half is None else (2 * c + half, 2 * self.chunks)

    def start(self, src=None):
        for c in range(self.chunks):
            ref = self.view(self.p.z, self.part(c))
            for side in range(2):
                own = ref if src is None else src(self.part(c))
                self.w.start(own, ref, self.sems[side][c], self.to[side], self.batch, self.cond)

    def step(self, s):
        for c in range(self.chunks):
            for side in range(2):
                self.hop(s, c, side)

    def hop(self, s, c, side):
        block = mod(self.p.z + (s if side else -s), SEQ)
        now = self.part(c, side if s == 4 else None)
        ref, sem, to = self.view(block, now), self.sems[side][c], self.to[side]
        self.w.arrive(ref, sem + s - 1, to, self.cond)
        if s < 4:
            later = self.view(block, self.part(c, side if s == 3 else None))
            self.w.start(later, later, sem + s, to, self.batch, self.cond)
        if self.on_chunk:
            self.on_chunk(block, now)


class Leap:
    def __init__(self, w, p, view, cond):
        self.w, self.p, self.view, self.cond = w, p, view, cond
        self.batch = Batch(w, cond)
        self.sems = [w.slot(4) for _ in range(2)]
        self.to = ((p.up, p.up2), (p.down, p.down2))

    def start(self):
        ref = self.view(self.p.z, None)
        for far in (1, 0):
            for side in range(2):
                to = self.to[side][far]
                self.w.start(ref, ref, self.sems[side] + far, to, self.batch, self.cond)

    def take(self, side, index, away, half=None):
        block = mod(self.p.z + (away if side else -away), SEQ)
        ref = self.view(block, half)
        self.w.arrive(ref, self.sems[side] + index, self.to[side][0], self.cond)
        return block, ref

    def relay(self):
        for side in range(2):
            block, ref = self.take(side, 1, 2)
            one, two = self.to[side]
            self.w.start(ref, ref, self.sems[side] + 2, one, self.batch, self.cond)
            ref = self.view(block, (side, 2))
            self.w.start(ref, ref, self.sems[side] + 3, two, self.batch, self.cond)

    def finish(self):
        for side in range(2):
            self.take(side, 0, 1)
            self.take(side, 2, 3)
            self.take(side, 3, 4, (side, 2))


class Share:
    def __init__(self, w, p, one_a, one_b):
        self.w, self.p, self.one_a, self.one_b = w, p, one_a, one_b
        self.s_a, self.s_b, self.batch, self.batch_b = w.slot(), w.slot(), Batch(w), Batch(w)
        self.ring_a = Ring(w, p, lambda j, part: one_a(j, p.d, part), 2)
        self.ring_o = Ring(w, p, lambda j, part: one_a(j, 1 - p.d, part), 2)
        self.ring_b = Ring(
            w, p, lambda j, part: one_b(j, p.d, part), 2, on_chunk=self.forward
        )

    def forward(self, block, part):
        ref = self.one_b(block, self.p.d, part)
        self.w.start(ref, ref, self.s_b, self.p.partner, self.batch_b)

    def start(self, own_a, own_b):
        p = self.p
        self.w.start(own_a(None), self.one_a(p.z, p.d, None), self.s_a, p.partner, self.batch)
        self.ring_b.start(own_b)
        self.ring_a.start(own_a)

    def open(self, own_b):
        p = self.p
        self.w.start(own_b(None), self.one_b(p.z, p.d, None), self.s_b, p.partner, self.batch_b)
        self.w.arrive(self.one_a(p.z, 1 - p.d, None), self.s_a, p.partner)
        self.ring_o.start()

    def finish(self):
        self.w.wait(self.w.recv.at[self.s_b], self.batch_b.rows)


class Spread:
    def __init__(self, w, p, view, low):
        self.w, self.p, self.view, self.low = w, p, view, low
        self.far, self.near = w.slot(8), w.slot()
        self.out = Batch(w, self.cond(p.chip))
        self.relayed = Batch(w, counts=p.others(48) if low else None)

    def cond(self, chip):
        return chip < 6 if self.low else None

    def start(self):
        w, p = self.w, self.p
        own = self.view(p.m)
        for off in range(1, 8):
            to = p.chip_id(p.peer(off))
            w.start(own, own, self.far + off, to, self.out, self.cond(p.chip))
        w.start(own, own, self.near, p.sibling, self.out, self.cond(p.chip))

    def relay(self):
        w, p = self.w, self.p
        for off in range(1, 8):
            src = p.source(off)
            ref = self.view(src * 2 + p.core)
            w.arrive(ref, self.far + off, p.chip_id(p.peer(off)), self.cond(src))
            w.start(ref, ref, self.near, p.sibling, self.relayed, self.cond(src))

    def finish(self):
        self.w.wait(self.w.recv.at[self.near], 48 * (6 if self.low else 8))


class Gather:
    def __init__(self, w, p, parts, near, far, low):
        self.w, self.p, self.parts, self.near, self.far, self.low = w, p, parts, near, far, low
        self.s_near, self.s_far = w.slot(8), w.slot()
        self.out = Batch(w, counts=((None, 6 * 48),) if low else None)
        self.relayed = Batch(w, counts=p.others(48) if low else None)

    def cond(self, chip):
        return chip < 6 if self.low else None

    def compute(self, chip, tile):
        def go():
            both = tile(chip)
            self.parts[0, chip] = both[:, :128].astype(BF)
            self.parts[1, chip] = both[:, 128:].astype(BF)

        guarded(self.cond(chip), go)
        self.w.start(
            self.parts.at[1 - self.p.core, chip],
            self.near.at[chip],
            self.s_near + chip,
            self.p.sibling,
            self.out,
            self.cond(chip),
        )

    def compute_all(self, tile):
        for off in (1, 2, 3, 4, 5, 6, 7, 0):
            self.compute(self.p.peer(off), tile)

    def relay(self):
        w, p = self.w, self.p
        for off in (1, 2, 3, 4, 5, 6, 7, 0):
            chip = p.peer(off)
            ref = self.near.at[chip]
            w.arrive(ref, self.s_near + chip, p.sibling, self.cond(chip))

            def go():
                total = ref[...].astype(F32) + self.parts[p.core, chip].astype(F32)
                self.near[chip] = total.astype(BF)

            guarded(self.cond(chip), go)
            if off:
                to = p.chip_id(chip)
                w.start(ref, self.far.at[off], self.s_far, to, self.relayed, self.cond(chip))

    def finish(self):
        w, p = self.w, self.p
        total = self.near[p.chip].astype(F32)
        w.arrive(self.far.at[1:8], self.s_far, p.sibling)
        for off in range(1, 8):
            total = total + self.far[off].astype(F32)
        return total


class Fold:
    def __init__(self, w, p, own, halves, fulls, chunks):
        self.w, self.p, self.own, self.halves, self.fulls = w, p, own, halves, fulls
        self.chunks, self.batch = chunks, Batch(w)
        self.sems = [[w.slot(4) for _ in range(chunks)] for _ in range(2)]
        self.to = (p.up, p.down)

    def start(self):
        for c in range(self.chunks):
            for side in range(2):
                src = self.own(mod(self.p.z + 4, SEQ), (2 * c + side, 2 * self.chunks))
                dst = self.halves(side, (c, self.chunks))
                self.w.start(src, dst, self.sems[side][c], self.to[side], self.batch)

    def step(self, s):
        for c in range(self.chunks):
            for side in range(2):
                self.hop(s, c, side)

    def hop(self, s, c, side):
        part, sem, to = (c, self.chunks), self.sems[side][c], self.to[side]
        block = mod(self.p.z + (s - 4 if side else 4 - s), SEQ)
        if s == 1:
            got, held = self.halves(side, part), self.own(block, (2 * c + side, 2 * self.chunks))
            self.w.arrive(got, sem, to)
            held[...] = (held[...].astype(F32) + got[...].astype(F32)).astype(BF)
            ref = self.own(block, part)
        else:
            ref, term = self.fulls(side, s - 2, part), self.own(block, part)
            self.w.arrive(ref, sem + s - 1, to)
            ref[...] = (ref[...].astype(F32) + term[...].astype(F32)).astype(BF)
        self.w.start(ref, self.fulls(side, s - 1, part), sem + s, to, self.batch)

    def finish(self):
        total = self.own(self.p.z, None)[...].astype(F32)
        for side in range(2):
            for c in range(self.chunks):
                ref = self.fulls(side, 2, (c, self.chunks))
                self.w.arrive(ref, self.sems[side][c] + 3, self.to[side])
            total = total + self.fulls(side, 2, None)[...].astype(F32)
        return total


class Twin:
    def __init__(self, w, p, ref):
        self.w, self.p, self.ref = w, p, ref
        self.slots, self.batch = (w.slot(), w.slot()), Batch(w)

    def rows(self, base, core):
        return self.ref.at[pl.ds(pl.multiple_of(base + core * 96, 32), 96)]

    def start(self):
        p = self.p
        to = self.rows(ROWS, p.core)
        self.w.start(self.rows(0, p.core), to, self.slots[0], p.partner, self.batch)

    def relay(self):
        p, ref = self.p, self.rows(ROWS, self.p.core)
        self.w.arrive(ref, self.slots[0], p.partner)
        self.w.start(ref, ref, self.slots[1], p.sibling, self.batch)

    def finish(self):
        self.w.arrive(self.rows(ROWS, 1 - self.p.core), self.slots[1], self.p.sibling)


def take_turns(*tasks):
    tasks = list(tasks)
    while tasks:
        for task in list(tasks):
            if next(task, "done") == "done":
                tasks.remove(task)


ORDER = (4, 3, -3, 2, -2, 1, -1, 0)


def kernel(
    q_in, k_in, v_in, c_in, rate_in,
    em_in, rm_in, e1_in, r1_in, e2_in, r2_in,
    mixed_ref, eu_ref, ru_ref, em1_ref, rm1_ref, ev_ref, rv_ref, ew_ref, rw_ref,
    q_ref, k_ref, v_ref, c_ref, rate_ref, em_ref, rm_ref, e1_ref, r1_ref, e2_ref, r2_ref,
    ef, rf, k_rows, r_rows, act_all, dz_all, score1, score3, act_b, slope, resid, qe, cr,
    parts, near, far, parts2, near2, far2, parts3, near3, far3, score2, aq, dzq,
    aq2, dzq2, g_e, g_r, half_buf, full_buf, swap_e, swap_r,
    w_e, w_r, send, recv, local,
):
    w, p = Wire(send, recv, ef), Place()
    m, z, d = p.m, p.z, p.d
    swaps = Batch(w)

    loads = {}
    for index, (src, dst) in enumerate(
        (
            (em_in, em_ref), (rm_in, rm_ref), (k_in, k_ref), (rate_in, rate_ref),
            (v_in, v_ref), (q_in, q_ref.at[0:ROWS]), (c_in, c_ref.at[0:ROWS]), (e1_in, e1_ref), (r1_in, r1_ref),
            (e2_in, e2_ref), (r2_in, r2_ref),
        )
    ):
        loads[index] = pltpu.make_async_copy(src, dst, local.at[index])
        loads[index].start()

    barrier = pltpu.get_barrier_semaphore()
    friends = [p.up, p.down, p.up2, p.down2, p.partner, p.sibling]
    friends += [p.chip_id(p.peer(off)) for off in range(1, 8)]
    for friend in friends:
        pl.semaphore_signal(barrier, inc=1, device_id=friend, device_id_type=MESH)
    pl.semaphore_wait(barrier, len(friends))

    def block_at(j, dd):
        return pl.multiple_of(j * 256 + dd * 128, 128)

    def share_e(full):
        def block(j, dd, part, columns):
            return full.at[span(block_at(j, dd), part, 128), columns]

        return Share(
            w,
            p,
            lambda j, dd, part: block(j, dd, part, slice(0, 256)),
            lambda j, dd, part: block(j, dd, part, slice(256, 512)),
        )

    def share_r(full):
        def block(j, dd, part, base):
            return full.at[span(base, part, 256), pl.ds(block_at(j, dd), 128)]

        return Share(
            w,
            p,
            lambda j, dd, part: block(j, dd, part, 0),
            lambda j, dd, part: block(j, dd, part, 256),
        )

    own_rows = pl.ds(pl.multiple_of(m * 16, 16), 16)

    def take_rows(out, rows_ref):
        def go():
            out[z] = rows_ref[own_rows, :]

        guarded(p.low, go)

    def rows_view(ref):
        return lambda j, part: ref.at[j, :, span(0, part, D)]

    share1, share2 = share_e(ef), share_r(rf)
    ring_k = Ring(w, p, rows_view(k_rows), cond=p.low)
    loads[0].wait()
    ef[pl.ds(block_at(z, d), 128), :] = em_ref[...].astype(BF)
    own1 = [lambda part: share1.one_a(z, d, part), lambda part: share1.one_b(z, d, part)]
    own2 = [lambda part: share2.one_a(z, d, part), lambda part: share2.one_b(z, d, part)]
    share1.start(*own1)
    loads[1].wait()
    rf[:, pl.ds(block_at(z, d), 128)] = rm_ref[...].astype(BF)
    share2.start(*own2)
    loads[2].wait()
    take_rows(k_rows, k_ref)
    ring_k.start()
    share1.open(own1[1])
    share2.open(own2[1])
    t_at = z * ROWS + lax.broadcasted_iota(jnp.int32, (ROWS, 128), 0)
    col = lax.broadcasted_iota(jnp.int32, (ROWS, 128), 1)
    s_at = (col // 16) * ROWS + m * 16 + lax.rem(col, 16)
    causal = t_at >= s_at
    eye = lax.broadcasted_iota(jnp.int32, (ROWS, ROWS), 0) == lax.broadcasted_iota(
        jnp.int32, (ROWS, ROWS), 1
    )
    loads[3].wait()
    rates = jnp.sum(jnp.where(eye, rate_ref[...], 0.0), axis=1, keepdims=True)


    def block_of(ref, block):
        return ref.at[:, pl.ds(pl.multiple_of(block * 128, 128), 128)]

    def wide(chip):
        return pl.ds(pl.multiple_of(chip * 256, 256), 256)

    spread1 = Spread(w, p, lambda b: block_of(score1, b), True)
    spread_r = Spread(w, p, lambda b: block_of(resid, b), False)
    spread3 = Spread(w, p, lambda b: block_of(score3, b), True)

    def score(rows_ref, others, out):
        def go():
            part = dot_nt(rows_ref[0:ROWS], others[...].reshape(128, D))
            block_of(out, m)[...] = jnp.where(causal, part, 0.0).astype(BF)

        guarded(p.low, go)

    def put(ref, columns, value):
        ref[:, z, :, columns] = value.astype(BF).reshape(12, 16, 256)

    def hidden_ring(ref, chunks):
        return Ring(w, p, lambda j, part: ref.at[span(0, part, 12), j], chunks)

    leap = Leap(w, p, rows_view(r_rows), p.low)
    ring_a, ring_z = hidden_ring(act_all, 3), hidden_ring(dz_all, 6)

    for s in range(1, 5):
        ring_k.step(s)
        for share in (share1, share2):
            share.ring_b.step(s)
        for share in (share1, share2):
            share.ring_a.step(s)
        for share in (share1, share2):
            share.ring_o.step(s)
    for index in (4, 5, 6):
        loads[index].wait()
    share1.finish()

    for n in range(2):
        columns = pl.ds(n * 256, 256)
        act, slope_n = gelu_both(dot(k_ref[...], ef[:, columns]))
        act_b[:, columns] = act.astype(BF)
        slope[:, columns] = slope_n
        put(act_all, columns, rates * act)

    ring_a.start()
    share2.finish()

    sum1 = Gather(w, p, parts, near, far, False)
    sum1.compute_all(lambda chip: dot(act_b[...], rf[:, wide(chip)]))
    sum1.relay()
    for n in range(2):
        columns = pl.ds(n * 256, 256)
        qe[:, columns] = dot(q_ref[0:ROWS], ef[:, columns])
    ring_a.step(1)
    recon = sum1.finish()
    block_of(resid, m)[...] = (
        block_of(k_ref, m)[...].astype(F32) + recon - block_of(v_ref, m)[...].astype(F32)
    ).astype(BF)
    spread_r.start()
    for n in range(2):
        columns = pl.ds(n * 256, 256)
        cr[:, columns] = dot_nt(c_ref[0:ROWS], rf[columns, :])
    ring_a.step(2)
    score(q_ref, k_rows, score1)
    spread_r.relay()
    ring_a.step(3)
    spread_r.finish()

    take_rows(r_rows, resid)
    for n in range(2):
        columns = pl.ds(n * 256, 256)
        d_hidden = dot_nt(resid[...], rf[columns, :]) * slope[:, columns]
        put(dz_all, columns, rates * d_hidden)
    ring_z.start()
    spread1.start()
    twin_q, twin_c = Twin(w, p, q_ref), Twin(w, p, c_ref)
    twin_c.start()
    ring_a.step(4)
    ring_z.step(1)
    spread1.relay()
    twin_q.start()
    ring_z.step(2)
    ring_z.step(3)
    leap.start()
    spread1.finish()
    twin_c.relay()
    ring_z.step(4)

    for n in range(2):
        columns = pl.ds(n * 256, 256)
        zq = qe[:, columns] - dot(score1[...], dz_all[:, :, :, columns].reshape(1536, 256))
        act, slope_n = gelu_both(zq)
        aq[:, columns] = act.astype(BF)
        slope[:, columns] = slope_n

    theirs = pl.ds(pl.multiple_of((1 - d) * 256, 256), 256)
    mine = pl.ds(pl.multiple_of(d * 256, 256), 256)
    s_aq, s_dzq = w.slot(), w.slot()
    w.start(aq.at[:, theirs], aq2.at[1], s_aq, p.partner, swaps)
    aq2[0] = aq[:, mine]
    sum2 = Gather(w, p, parts2, near2, far2, True)
    sum2.compute_all(
        lambda chip: dot_nt(aq[...], act_all[pl.ds(2 * chip, 2)].reshape(256, HID))
    )

    def fold_of(ref, k):
        return Fold(
            w,
            p,
            lambda j, part: ref.at[j, span(0, part, 256)],
            lambda side, part: half_buf.at[2 * k + side, span(0, part, 128)],
            lambda side, s, part: full_buf.at[2 * k + side, s, span(0, part, 256)],
            4,
        )

    fold_r, fold_e = fold_of(g_r, 0), fold_of(g_e, 1)
    leap.relay()
    twin_c.finish()
    w.arrive(aq2.at[1], s_aq, p.partner)
    for i, off in enumerate(ORDER):
        block = mod(z + off, SEQ)
        g_r[block] = dot_tn(aq2[...].reshape(2 * ROWS, 256), c_ref[:, wide(block)]).astype(BF)
        if i == 0:
            fold_r.start()
    leap.finish()
    score(c_ref, r_rows, score3)
    spread3.start()
    twin_q.relay()
    fold_r.step(1)
    spread3.relay()
    fold_r.step(2)
    spread3.finish()
    for n in range(2):
        columns = pl.ds(n * 256, 256)
        d_act = cr[:, columns] - dot(score3[...], act_all[:, :, :, columns].reshape(1536, 256))
        dzq[:, columns] = (d_act * slope[:, columns]).astype(BF)
    w.start(dzq.at[:, theirs], dzq2.at[1], s_dzq, p.partner, swaps)
    dzq2[0] = dzq[:, mine]
    sum2.relay()
    fold_r.step(3)
    twin_q.finish()
    w.arrive(dzq2.at[1], s_dzq, p.partner)
    for i, off in enumerate(ORDER):
        block = mod(z + off, SEQ)
        g_e[block] = dot_tn(q_ref[:, wide(block)], dzq2[...].reshape(2 * ROWS, 256)).astype(BF)
        if i == 0:
            fold_e.start()

    for index in (7, 8, 9, 10):
        loads[index].wait()
    share3, share4 = share_e(ew_ref), share_r(rw_ref)
    def optimizer(is_e, half, grad):
        refs = (
            (em_ref, e1_ref, e2_ref, eu_ref, em1_ref, ev_ref, w_e)
            if is_e
            else (rm_ref, r1_ref, r2_ref, ru_ref, rm1_ref, rv_ref, w_r)
        )
        at = pl.ds(pl.multiple_of(256 * half, 256), 256)
        at = (slice(None), at) if is_e else (at, slice(None))
        outs = adam_update(refs[0][at], refs[1][at], refs[2][at], grad)
        refs[3][at], refs[4][at], refs[5][at] = outs
        refs[6][at] = outs[0].astype(BF)

    def matrix(is_e, fold, swap, first):
        for s in range(first, 4):
            fold.step(s)
            yield
        total = fold.finish()
        for dd in range(2):
            at = slice(128 * dd, 128 * dd + 128)
            swap[dd] = (total[at] if is_e else total[:, at]).astype(BF)
        slot = w.slot()
        w.start(swap.at[1 - d], swap.at[2], slot, p.partner, swaps)
        optimizer(is_e, d, swap[d].astype(F32))
        yield
        w.arrive(swap.at[2], slot, p.partner)
        optimizer(is_e, 1 - d, swap[2].astype(F32))
        share = share3 if is_e else share4
        own = w_e if is_e else w_r

        def own_a(part):
            return own.at[span(0, part, 128), 0:256] if is_e else own.at[span(0, part, 256)]

        def own_b(part):
            return own.at[span(0, part, 128), 256:512] if is_e else own.at[span(256, part, 256)]

        share.start(own_a, own_b)
        keeps = []
        for src, dst in ((own_a, share.one_a), (own_b, share.one_b)):
            index = 11 + len(keeps) + 2 * is_e
            keeps.append(pltpu.make_async_copy(src(None), dst(z, d, None), local.at[index]))
            keeps[-1].start()
        yield
        share.open(own_b)
        for s in range(1, 5):
            yield
            share.ring_b.step(s)
            share.ring_a.step(s)
            share.ring_o.step(s)
        for keep in keeps:
            keep.wait()
        yield
        share.finish()

    def output():
        pl.when(p.low)(own_score)
        pl.when(jnp.logical_not(p.low))(lambda: clear(score2, r_rows))
        sum3 = Gather(w, p, parts3, near3, far3, False)
        sum3.compute_all(mixed_tile)
        yield
        sum3.relay()
        yield
        mixed_ref[...] = (block_of(q_ref, m)[0:ROWS].astype(F32) + sum3.finish()).astype(BF)

    def own_score():
        score2[...] = jnp.where(causal, sum2.finish(), 0.0).astype(BF)

    def mixed_tile(chip):
        first = dot(aq[...], rf[:, wide(chip)])
        return first - dot(score2[...], r_rows[:, :, wide(chip)].reshape(128, 256))

    take_turns(
        matrix(False, fold_r, swap_r, 4),
        matrix(True, fold_e, swap_e, 1),
        output(),
    )
    w.drain()


def clear(*refs):
    for ref in refs:
        ref[...] = jnp.zeros(ref.shape, ref.dtype)


def pass_on(*refs):
    *arrays, sems = refs
    count = len(arrays) // 3
    ins, outs = [], []
    for src, dst, held in zip(arrays[:count], arrays[count : 2 * count], arrays[2 * count :]):
        pieces = 4 if src.shape[0] * src.shape[1] > 100_000 else 1
        size = src.shape[0] // pieces
        for piece in range(pieces):
            rows = pl.ds(piece * size, size)
            index = len(ins)
            ins.append(pltpu.make_async_copy(src.at[rows], held.at[rows], sems.at[0, index]))
            outs.append(pltpu.make_async_copy(held.at[rows], dst.at[rows], sems.at[1, index]))
            ins[-1].start()
    for copy_in, copy_out in zip(ins, outs):
        copy_in.wait()
        copy_out.start()
    for copy_out in outs:
        copy_out.wait()


def body(
    query_rows, key_rows, value_rows, cotangent, inner_rate,
    expand_master, reduce_master, expand_first, reduce_first, expand_second, reduce_second,
):
    vmem = pl.BlockSpec(memory_space=pltpu.VMEM)
    hbm = pl.BlockSpec(memory_space=pl.ANY)
    e_shape, r_shape = expand_master.shape, reduce_master.shape

    def bf(*shape):
        return pltpu.VMEM(shape, BF)

    def f32(*shape):
        return pltpu.VMEM(shape, F32)

    outs = pl.pallas_call(
        kernel,
        out_shape=[
            jax.ShapeDtypeStruct((ROWS, 128), BF),
            jax.ShapeDtypeStruct(e_shape, F32),
            jax.ShapeDtypeStruct(r_shape, F32),
            jax.ShapeDtypeStruct(e_shape, F32),
            jax.ShapeDtypeStruct(r_shape, F32),
            jax.ShapeDtypeStruct(e_shape, F32),
            jax.ShapeDtypeStruct(r_shape, F32),
            jax.ShapeDtypeStruct((D, HID), BF),
            jax.ShapeDtypeStruct((HID, D), BF),
        ],
        in_specs=[hbm] * 11,
        out_specs=[vmem] * 7 + [hbm] * 2,
        scratch_shapes=[
            bf(2 * ROWS, D), bf(ROWS, D), bf(ROWS, D), bf(2 * ROWS, D), f32(1, ROWS),
            f32(*e_shape), f32(*r_shape), f32(*e_shape), f32(*r_shape), f32(*e_shape), f32(*r_shape),
            bf(D, HID), bf(HID, D),
            bf(SEQ, 16, D), bf(SEQ, 16, D),
            bf(12, SEQ, 16, HID), bf(12, SEQ, 16, HID),
            bf(ROWS, 1536), bf(ROWS, 1536),
            bf(ROWS, HID), f32(ROWS, HID),
            bf(ROWS, D), f32(ROWS, HID), f32(ROWS, HID),
            bf(2, 8, ROWS, 128), bf(8, ROWS, 128), bf(8, ROWS, 128),
            bf(2, 6, ROWS, 128), bf(6, ROWS, 128), bf(8, ROWS, 128),
            bf(2, 8, ROWS, 128), bf(8, ROWS, 128), bf(8, ROWS, 128),
            bf(ROWS, 128), bf(ROWS, HID), bf(ROWS, HID),
            bf(2, ROWS, 256), bf(2, ROWS, 256),
            bf(SEQ, 256, 256), bf(SEQ, 256, 256),
            bf(4, 128, 256), bf(4, 3, 256, 256),
            bf(3, 128, 256), bf(3, 256, 128),
            bf(128, HID), bf(HID, 128),
            pltpu.SemaphoreType.DMA((N_SEND,)),
            pltpu.SemaphoreType.DMA((N_RECV,)),
            pltpu.SemaphoreType.DMA((16,)),
        ],
        compiler_params=pltpu.CompilerParams(
            collective_id=0, has_side_effects=True, vmem_limit_bytes=56 * 1024 * 1024
        ),
        cost_estimate=pl.CostEstimate(
            flops=5_000_000_000, bytes_accessed=12_000_000, transcendentals=400_000
        ),
    )(
        query_rows[0], key_rows[0], value_rows[0], cotangent[0], inner_rate,
        expand_master, reduce_master, expand_first, reduce_first, expand_second, reduce_second,
    )
    outs = pl.pallas_call(
        pass_on,
        out_shape=[jax.ShapeDtypeStruct(out.shape, out.dtype) for out in outs],
        in_specs=[hbm] * 9,
        out_specs=[hbm] * 9,
        scratch_shapes=[pltpu.VMEM(out.shape, out.dtype) for out in outs]
        + [pltpu.SemaphoreType.DMA((2, 16))],
        compiler_params=pltpu.CompilerParams(vmem_limit_bytes=60 * 1024 * 1024),
        cost_estimate=pl.CostEstimate(flops=0, bytes_accessed=12_000_000, transcendentals=0),
    )(*outs)
    return (outs[0][None], *outs[1:])


def solution(mesh):
    in_specs = (
        P("dp", "seq", None),
        P("dp", "seq", None),
        P("dp", "seq", None),
        P("dp", "seq", None),
        P("dp", "seq"),
        P(("seq", "dp"), "mp"),
        P("mp", ("seq", "dp")),
        P(("seq", "dp"), "mp"),
        P("mp", ("seq", "dp")),
        P(("seq", "dp"), "mp"),
        P("mp", ("seq", "dp")),
    )
    out_specs = (
        P("dp", "seq", "mp"),
        P(("seq", "dp"), "mp"),
        P("mp", ("seq", "dp")),
        P(("seq", "dp"), "mp"),
        P("mp", ("seq", "dp")),
        P(("seq", "dp"), "mp"),
        P("mp", ("seq", "dp")),
        P(None, "mp"),
        P("mp", None),
    )
    return jax.shard_map(body, mesh=mesh, in_specs=in_specs, out_specs=out_specs, check_vma=False)
```

```python
import jax
import jax.numpy as jnp
from jax import lax
from jax.experimental import pallas as pl
from jax.experimental.pallas import tpu as pltpu
from jax.sharding import PartitionSpec as P

STEP = 1000
MESH = pl.DeviceIdType.MESH
F32 = jnp.float32
BF = jnp.bfloat16

gelu_scale = 0.7978845608028654
gelu_cubic = 0.044715
beta_first = 0.9
beta_second = 0.999
learn_rate = 0.001
weight_decay = 0.1
adam_eps = 1e-08

SEQ, DP, MP = 8, 2, 16
ROWS, D, HID = 192, 2048, 512
N_RECV, N_SEND = 314, 41


def gelu_both(value):
    inner = jnp.tanh(gelu_scale * (value + gelu_cubic * value * value * value))
    act = 0.5 * value * (1.0 + inner)
    slope = 0.5 * (1.0 + inner) + 0.5 * value * (1.0 - inner * inner) * gelu_scale * (
        1.0 + 3.0 * gelu_cubic * value * value
    )
    return act, slope


def adam_update(master, first, second, grad):
    momentum = beta_first * first + (1.0 - beta_first) * grad
    variance = beta_second * second + (1.0 - beta_second) * grad * grad
    first_corr = 1.0 - beta_first**STEP
    second_corr = 1.0 - beta_second**STEP
    updated = master - learn_rate * (
        momentum / first_corr / (jnp.sqrt(variance / second_corr) + adam_eps)
        + weight_decay * master
    )
    return (updated, momentum, variance)


def dot(a, b):
    return jnp.dot(a, b, preferred_element_type=F32)


def dot_nt(a, b):
    return lax.dot_general(a, b, (((1,), (1,)), ((), ())), preferred_element_type=F32)


def dot_tn(a, b):
    return lax.dot_general(a, b, (((0,), (0,)), ((), ())), preferred_element_type=F32)


def mod(a, n):
    return lax.rem(a + 2 * n, n)


class Batch:
    def __init__(self, w, cond=None, counts=None):
        self.sem, self.rows, self.cond, self.counts = len(w.batches), 0, cond, counts
        w.batches.append(self)
        assert self.sem < N_SEND


class Wire:
    def __init__(self, send, recv, dummy):
        self.send, self.recv, self.dummy = send, recv, dummy
        self.count, self.batches = 0, []

    def slot(self, count=1):
        self.count += count
        assert self.count <= N_RECV
        return self.count - count

    def copy(self, src, dst, slot, to, out=0):
        return pltpu.make_async_remote_copy(
            src_ref=src,
            dst_ref=dst,
            send_sem=self.send.at[out],
            recv_sem=self.recv.at[slot],
            device_id=to,
            device_id_type=MESH,
        )

    def start(self, src, dst, slot, to, batch, cond=None):
        guarded(cond, lambda: self.copy(src, dst, slot, to, batch.sem).start())
        size = 1
        for extent in src.shape:
            size *= extent
        batch.rows += size // HID

    def arrive(self, dst, slot, to, cond=None):
        guarded(cond, lambda: self.copy(dst, dst, slot, to).wait_recv())

    def wait(self, sem, rows):
        ref = self.dummy.at[0:rows]
        pltpu.make_async_copy(ref, ref, sem).wait()

    def drain(self):
        for batch in self.batches:
            if not batch.rows:
                continue
            for cond, rows in batch.counts or ((batch.cond, batch.rows),):
                guarded(cond, lambda: self.wait(self.send.at[batch.sem], rows))


def guarded(cond, go):
    if cond is None:
        go()
    else:
        pl.when(cond)(go)


class Place:
    def __init__(self):
        self.m = lax.axis_index("mp")
        self.z = lax.axis_index("seq")
        self.d = lax.axis_index("dp")
        self.core = lax.rem(self.m, 2)
        self.chip = self.m // 2
        self.sibling = {"mp": self.chip * 2 + 1 - self.core}
        self.partner = {"dp": 1 - self.d}
        self.up = {"seq": mod(self.z + 1, SEQ)}
        self.down = {"seq": mod(self.z - 1, SEQ)}
        self.up2 = {"seq": mod(self.z + 2, SEQ)}
        self.down2 = {"seq": mod(self.z - 2, SEQ)}
        self.low = self.chip < 6

    def peer(self, off):
        return lax.rem(self.chip + off, 8)

    def source(self, off):
        return lax.rem(self.chip + 8 - off, 8)

    def others(self, rows):
        return ((self.low, 5 * rows), (jnp.logical_not(self.low), 6 * rows))

    def chip_id(self, chip):
        return {"mp": chip * 2 + self.core}


def span(base, part, size):
    if part is None:
        return pl.ds(base, size)
    i, n = part
    return pl.ds(base + i * (size // n), size // n)


class Ring:
    def __init__(self, w, p, view, chunks=1, cond=None, on_chunk=None, like=None):
        self.w, self.p, self.view, self.chunks = w, p, view, chunks
        self.cond, self.on_chunk, self.batch = cond, on_chunk, Batch(w, cond)
        self.sems = like.sems if like else [[w.slot(4) for _ in range(chunks)] for _ in range(2)]
        self.to = (p.up, p.down)

    def part(self, c, half=None):
        return (c, self.chunks) if half is None else (2 * c + half, 2 * self.chunks)

    def start(self, src=None):
        for c in range(self.chunks):
            ref = self.view(self.p.z, self.part(c))
            for side in range(2):
                own = ref if src is None else src(self.part(c))
                self.w.start(own, ref, self.sems[side][c], self.to[side], self.batch, self.cond)

    def step(self, s):
        for c in range(self.chunks):
            for side in range(2):
                self.hop(s, c, side)

    def hop(self, s, c, side):
        block = mod(self.p.z + (s if side else -s), SEQ)
        now = self.part(c, side if s == 4 else None)
        ref, sem, to = self.view(block, now), self.sems[side][c], self.to[side]
        self.w.arrive(ref, sem + s - 1, to, self.cond)
        if s < 4:
            later = self.view(block, self.part(c, side if s == 3 else None))
            self.w.start(later, later, sem + s, to, self.batch, self.cond)
        if self.on_chunk:
            self.on_chunk(block, now)


class Leap:
    def __init__(self, w, p, view, cond):
        self.w, self.p, self.view, self.cond = w, p, view, cond
        self.batch = Batch(w, cond)
        self.sems = [w.slot(4) for _ in range(2)]
        self.to = ((p.up, p.up2), (p.down, p.down2))

    def start(self):
        ref = self.view(self.p.z, None)
        for far in (1, 0):
            for side in range(2):
                to = self.to[side][far]
                self.w.start(ref, ref, self.sems[side] + far, to, self.batch, self.cond)

    def take(self, side, index, away, half=None):
        block = mod(self.p.z + (away if side else -away), SEQ)
        ref = self.view(block, half)
        self.w.arrive(ref, self.sems[side] + index, self.to[side][0], self.cond)
        return block, ref

    def relay(self):
        for side in range(2):
            block, ref = self.take(side, 1, 2)
            one, two = self.to[side]
            self.w.start(ref, ref, self.sems[side] + 2, one, self.batch, self.cond)
            ref = self.view(block, (side, 2))
            self.w.start(ref, ref, self.sems[side] + 3, two, self.batch, self.cond)

    def finish(self):
        for side in range(2):
            self.take(side, 0, 1)
            self.take(side, 2, 3)
            self.take(side, 3, 4, (side, 2))


class Share:
    def __init__(self, w, p, one_a, one_b, like=None):
        self.w, self.p, self.one_a, self.one_b = w, p, one_a, one_b
        self.s_a, self.s_b = (like.s_a, like.s_b) if like else (w.slot(), w.slot())
        self.batch, self.batch_b = Batch(w), Batch(w)
        earlier = (like.ring_a, like.ring_o, like.ring_b) if like else (None, None, None)
        self.ring_a = Ring(w, p, lambda j, part: one_a(j, p.d, part), 2, like=earlier[0])
        self.ring_o = Ring(w, p, lambda j, part: one_a(j, 1 - p.d, part), 2, like=earlier[1])
        self.ring_b = Ring(
            w, p, lambda j, part: one_b(j, p.d, part), 2, on_chunk=self.forward, like=earlier[2]
        )

    def forward(self, block, part):
        ref = self.one_b(block, self.p.d, part)
        self.w.start(ref, ref, self.s_b, self.p.partner, self.batch_b)

    def start(self, own_a, own_b):
        p = self.p
        self.w.start(own_a(None), self.one_a(p.z, p.d, None), self.s_a, p.partner, self.batch)
        self.ring_b.start(own_b)
        self.ring_a.start(own_a)

    def open(self, own_b):
        p = self.p
        self.w.start(own_b(None), self.one_b(p.z, p.d, None), self.s_b, p.partner, self.batch_b)
        self.w.arrive(self.one_a(p.z, 1 - p.d, None), self.s_a, p.partner)
        self.ring_o.start()

    def finish(self):
        self.w.wait(self.w.recv.at[self.s_b], self.batch_b.rows)


class Spread:
    def __init__(self, w, p, view, low):
        self.w, self.p, self.view, self.low = w, p, view, low
        self.far, self.near = w.slot(8), w.slot()
        self.out = Batch(w, self.cond(p.chip))
        self.relayed = Batch(w, counts=p.others(48) if low else None)

    def cond(self, chip):
        return chip < 6 if self.low else None

    def start(self):
        w, p = self.w, self.p
        own = self.view(p.m)
        for off in range(1, 8):
            to = p.chip_id(p.peer(off))
            w.start(own, own, self.far + off, to, self.out, self.cond(p.chip))
        w.start(own, own, self.near, p.sibling, self.out, self.cond(p.chip))

    def relay(self):
        w, p = self.w, self.p
        for off in range(1, 8):
            src = p.source(off)
            ref = self.view(src * 2 + p.core)
            w.arrive(ref, self.far + off, p.chip_id(p.peer(off)), self.cond(src))
            w.start(ref, ref, self.near, p.sibling, self.relayed, self.cond(src))

    def finish(self):
        self.w.wait(self.w.recv.at[self.near], 48 * (6 if self.low else 8))


class Gather:
    def __init__(self, w, p, parts, near, far, low):
        self.w, self.p, self.parts, self.near, self.far, self.low = w, p, parts, near, far, low
        self.s_near, self.s_far = w.slot(8), w.slot()
        self.out = Batch(w, counts=((None, 6 * 48),) if low else None)
        self.relayed = Batch(w, counts=p.others(48) if low else None)

    def cond(self, chip):
        return chip < 6 if self.low else None

    def compute(self, chip, tile):
        def go():
            both = tile(chip)
            self.parts[0, chip] = both[:, :128].astype(BF)
            self.parts[1, chip] = both[:, 128:].astype(BF)

        guarded(self.cond(chip), go)
        self.w.start(
            self.parts.at[1 - self.p.core, chip],
            self.near.at[chip],
            self.s_near + chip,
            self.p.sibling,
            self.out,
            self.cond(chip),
        )

    def compute_all(self, tile):
        for off in (1, 2, 3, 4, 5, 6, 7, 0):
            self.compute(self.p.peer(off), tile)

    def relay(self):
        w, p = self.w, self.p
        for off in (1, 2, 3, 4, 5, 6, 7, 0):
            chip = p.peer(off)
            ref = self.near.at[chip]
            w.arrive(ref, self.s_near + chip, p.sibling, self.cond(chip))

            def go():
                total = ref[...].astype(F32) + self.parts[p.core, chip].astype(F32)
                self.near[chip] = total.astype(BF)

            guarded(self.cond(chip), go)
            if off:
                to = p.chip_id(chip)
                w.start(ref, self.far.at[off], self.s_far, to, self.relayed, self.cond(chip))

    def finish(self):
        w, p = self.w, self.p
        total = self.near[p.chip].astype(F32)
        w.arrive(self.far.at[1:8], self.s_far, p.sibling)
        for off in range(1, 8):
            total = total + self.far[off].astype(F32)
        return total


class Fold:
    def __init__(self, w, p, own, halves, fulls, chunks):
        self.w, self.p, self.own, self.halves, self.fulls = w, p, own, halves, fulls
        self.chunks, self.batch = chunks, Batch(w)
        self.sems = [[w.slot(4) for _ in range(chunks)] for _ in range(2)]
        self.to = (p.up, p.down)

    def start(self):
        for c in range(self.chunks):
            for side in range(2):
                src = self.own(mod(self.p.z + 4, SEQ), (2 * c + side, 2 * self.chunks))
                dst = self.halves(side, (c, self.chunks))
                self.w.start(src, dst, self.sems[side][c], self.to[side], self.batch)

    def step(self, s):
        for c in range(self.chunks):
            for side in range(2):
                self.hop(s, c, side)

    def hop(self, s, c, side):
        part, sem, to = (c, self.chunks), self.sems[side][c], self.to[side]
        block = mod(self.p.z + (s - 4 if side else 4 - s), SEQ)
        if s == 1:
            got, held = self.halves(side, part), self.own(block, (2 * c + side, 2 * self.chunks))
            self.w.arrive(got, sem, to)
            held[...] = (held[...].astype(F32) + got[...].astype(F32)).astype(BF)
            ref = self.own(block, part)
        else:
            ref, term = self.fulls(side, s - 2, part), self.own(block, part)
            self.w.arrive(ref, sem + s - 1, to)
            ref[...] = (ref[...].astype(F32) + term[...].astype(F32)).astype(BF)
        self.w.start(ref, self.fulls(side, s - 1, part), sem + s, to, self.batch)

    def finish(self):
        total = self.own(self.p.z, None)[...].astype(F32)
        for side in range(2):
            for c in range(self.chunks):
                ref = self.fulls(side, 2, (c, self.chunks))
                self.w.arrive(ref, self.sems[side][c] + 3, self.to[side])
            total = total + self.fulls(side, 2, None)[...].astype(F32)
        return total


class Twin:
    def __init__(self, w, p, ref):
        self.w, self.p, self.ref = w, p, ref
        self.slots, self.batch = (w.slot(), w.slot()), Batch(w)

    def rows(self, base, core):
        return self.ref.at[pl.ds(pl.multiple_of(base + core * 96, 32), 96)]

    def start(self):
        p = self.p
        to = self.rows(ROWS, p.core)
        self.w.start(self.rows(0, p.core), to, self.slots[0], p.partner, self.batch)

    def relay(self):
        p, ref = self.p, self.rows(ROWS, self.p.core)
        self.w.arrive(ref, self.slots[0], p.partner)
        self.w.start(ref, ref, self.slots[1], p.sibling, self.batch)

    def finish(self):
        self.w.arrive(self.rows(ROWS, 1 - self.p.core), self.slots[1], self.p.sibling)


def take_turns(*tasks):
    tasks = list(tasks)
    while tasks:
        for task in list(tasks):
            if next(task, "done") == "done":
                tasks.remove(task)


ORDER = (4, 3, -3, 2, -2, 1, -1, 0)


def kernel(
    q_in, k_in, v_in, c_in, rate_in,
    em_in, rm_in, e1_in, r1_in, e2_in, r2_in,
    mixed_ref, eu_ref, ru_ref, em1_ref, rm1_ref, ev_ref, rv_ref, ew_ref, rw_ref,
    q_ref, k_ref, v_ref, c_ref, rate_ref, em_ref, rm_ref, e1_ref, r1_ref, e2_ref, r2_ref,
    ef, rf, k_rows, r_rows, act_all, dz_all, score1, score3, act_b, slope, resid, qe, cr,
    parts, near, far, parts2, near2, far2, parts3, near3, far3, score2, aq, dzq,
    aq2, dzq2, g_e, g_r, half_buf, full_buf, swap_e, swap_r,
    w_e, w_r, send, recv, local,
):
    w, p = Wire(send, recv, ef), Place()
    m, z, d = p.m, p.z, p.d
    swaps = Batch(w)

    loads = {}
    for index, (src, dst) in enumerate(
        (
            (em_in, em_ref), (rm_in, rm_ref), (k_in, k_ref), (rate_in, rate_ref),
            (v_in, v_ref), (q_in, q_ref.at[0:ROWS]), (c_in, c_ref.at[0:ROWS]), (e1_in, e1_ref), (r1_in, r1_ref),
            (e2_in, e2_ref), (r2_in, r2_ref),
        )
    ):
        loads[index] = pltpu.make_async_copy(src, dst, local.at[index])
        loads[index].start()

    barrier = pltpu.get_barrier_semaphore()
    friends = [p.up, p.down, p.up2, p.down2, p.partner, p.sibling]
    friends += [p.chip_id(p.peer(off)) for off in range(1, 8)]
    for friend in friends:
        pl.semaphore_signal(barrier, inc=1, device_id=friend, device_id_type=MESH)
    pl.semaphore_wait(barrier, len(friends))

    def block_at(j, dd):
        return pl.multiple_of(j * 256 + dd * 128, 128)

    def share_e(full, like=None):
        def block(j, dd, part, columns):
            return full.at[span(block_at(j, dd), part, 128), columns]

        return Share(
            w,
            p,
            lambda j, dd, part: block(j, dd, part, slice(0, 256)),
            lambda j, dd, part: block(j, dd, part, slice(256, 512)),
            like,
        )

    def share_r(full, like=None):
        def block(j, dd, part, base, size):
            return full.at[span(base, part, size), pl.ds(block_at(j, dd), 128)]

        return Share(
            w,
            p,
            lambda j, dd, part: block(j, dd, part, 0, 192),
            lambda j, dd, part: block(j, dd, part, 192, 320),
            like,
        )

    own_rows = pl.ds(pl.multiple_of(m * 16, 16), 16)

    def take_rows(out, rows_ref):
        def go():
            out[z] = rows_ref[own_rows, :]

        guarded(p.low, go)

    def rows_view(ref):
        return lambda j, part: ref.at[j, :, span(0, part, D)]

    share1, share2 = share_e(ef), share_r(rf)
    ring_k = Ring(w, p, rows_view(k_rows), cond=p.low)
    loads[0].wait()
    ef[pl.ds(block_at(z, d), 128), :] = em_ref[...].astype(BF)
    own1 = [lambda part: share1.one_a(z, d, part), lambda part: share1.one_b(z, d, part)]
    own2 = [lambda part: share2.one_a(z, d, part), lambda part: share2.one_b(z, d, part)]
    share1.start(*own1)
    loads[1].wait()
    rf[:, pl.ds(block_at(z, d), 128)] = rm_ref[...].astype(BF)
    share2.start(*own2)
    share1.open(own1[1])
    share2.open(own2[1])
    t_at = z * ROWS + lax.broadcasted_iota(jnp.int32, (ROWS, 128), 0)
    col = lax.broadcasted_iota(jnp.int32, (ROWS, 128), 1)
    s_at = (col // 16) * ROWS + m * 16 + lax.rem(col, 16)
    causal = t_at >= s_at
    eye = lax.broadcasted_iota(jnp.int32, (ROWS, ROWS), 0) == lax.broadcasted_iota(
        jnp.int32, (ROWS, ROWS), 1
    )
    loads[3].wait()
    rates = jnp.sum(jnp.where(eye, rate_ref[...], 0.0), axis=1, keepdims=True)


    def block_of(ref, block):
        return ref.at[:, pl.ds(pl.multiple_of(block * 128, 128), 128)]

    def wide(chip):
        return pl.ds(pl.multiple_of(chip * 256, 256), 256)

    spread1 = Spread(w, p, lambda b: block_of(score1, b), True)
    spread_r = Spread(w, p, lambda b: block_of(resid, b), False)
    spread3 = Spread(w, p, lambda b: block_of(score3, b), True)

    def score(rows_ref, others, out):
        def go():
            part = dot_nt(rows_ref[0:ROWS], others[...].reshape(128, D))
            block_of(out, m)[...] = jnp.where(causal, part, 0.0).astype(BF)

        guarded(p.low, go)

    def put(ref, columns, value):
        ref[:, z, :, columns] = value.astype(BF).reshape(12, 16, 256)

    def hidden_ring(ref, chunks):
        return Ring(w, p, lambda j, part: ref.at[span(0, part, 12), j], chunks)

    leap = Leap(w, p, rows_view(r_rows), p.low)
    ring_a, ring_z = hidden_ring(act_all, 3), hidden_ring(dz_all, 6)

    for s in range(1, 5):
        for share in (share1, share2):
            share.ring_b.step(s)
        for share in (share1, share2):
            share.ring_a.step(s)
        for share in (share1, share2):
            share.ring_o.step(s)
    for index in (2, 4, 5, 6):
        loads[index].wait()
    share1.finish()

    for n in range(2):
        columns = pl.ds(n * 256, 256)
        act, slope_n = gelu_both(dot(k_ref[...], ef[:, columns]))
        act_b[:, columns] = act.astype(BF)
        slope[:, columns] = slope_n
        put(act_all, columns, rates * act)

    ring_a.start()
    take_rows(k_rows, k_ref)
    ring_k.start()
    share2.finish()

    sum1 = Gather(w, p, parts, near, far, False)
    sum1.compute_all(lambda chip: dot(act_b[...], rf[:, wide(chip)]))
    sum1.relay()
    for n in range(2):
        columns = pl.ds(n * 256, 256)
        qe[:, columns] = dot(q_ref[0:ROWS], ef[:, columns])
    ring_a.step(1)
    ring_k.step(1)
    recon = sum1.finish()
    block_of(resid, m)[...] = (
        block_of(k_ref, m)[...].astype(F32) + recon - block_of(v_ref, m)[...].astype(F32)
    ).astype(BF)
    spread_r.start()
    for n in range(2):
        columns = pl.ds(n * 256, 256)
        cr[:, columns] = dot_nt(c_ref[0:ROWS], rf[columns, :])
    ring_a.step(2)
    ring_k.step(2)
    spread_r.relay()
    ring_a.step(3)
    ring_k.step(3)
    spread_r.finish()

    take_rows(r_rows, resid)
    for n in range(2):
        columns = pl.ds(n * 256, 256)
        d_hidden = dot_nt(resid[...], rf[columns, :]) * slope[:, columns]
        put(dz_all, columns, rates * d_hidden)
    ring_z.start()
    twin_q, twin_c = Twin(w, p, q_ref), Twin(w, p, c_ref)
    twin_c.start()
    ring_a.step(4)
    ring_k.step(4)
    score(q_ref, k_rows, score1)
    spread1.start()
    ring_z.step(1)
    twin_q.start()
    ring_z.step(2)
    spread1.relay()
    ring_z.step(3)
    leap.start()
    spread1.finish()
    twin_c.relay()
    ring_z.step(4)

    theirs = pl.ds(pl.multiple_of((1 - d) * 256, 256), 256)
    mine = pl.ds(pl.multiple_of(d * 256, 256), 256)
    s_aq, s_dzq = w.slot(), w.slot()
    for columns in (theirs, mine):
        zq = qe[:, columns] - dot(score1[...], dz_all[:, :, :, columns].reshape(1536, 256))
        act, slope_n = gelu_both(zq)
        aq[:, columns] = act.astype(BF)
        slope[:, columns] = slope_n
        if columns is theirs:
            w.start(aq.at[:, theirs], aq2.at[1], s_aq, p.partner, swaps)
    aq2[0] = aq[:, mine]

    sum2 = Gather(w, p, parts2, near2, far2, True)
    sum2.compute_all(
        lambda chip: dot_nt(aq[...], act_all[pl.ds(2 * chip, 2)].reshape(256, HID))
    )

    def fold_of(ref, k):
        return Fold(
            w,
            p,
            lambda j, part: ref.at[j, span(0, part, 256)],
            lambda side, part: half_buf.at[2 * k + side, span(0, part, 128)],
            lambda side, s, part: full_buf.at[2 * k + side, s, span(0, part, 256)],
            4,
        )

    fold_r, fold_e = fold_of(g_r, 0), fold_of(g_e, 1)
    leap.relay()
    twin_c.finish()
    w.arrive(aq2.at[1], s_aq, p.partner)
    for i, off in enumerate(ORDER):
        block = mod(z + off, SEQ)
        g_r[block] = dot_tn(aq2[...].reshape(2 * ROWS, 256), c_ref[:, wide(block)]).astype(BF)
        if i == 0:
            fold_r.start()
    leap.finish()
    score(c_ref, r_rows, score3)
    spread3.start()
    twin_q.relay()
    fold_r.step(1)
    spread3.relay()
    fold_r.step(2)
    spread3.finish()
    for columns in (theirs, mine):
        d_act = cr[:, columns] - dot(score3[...], act_all[:, :, :, columns].reshape(1536, 256))
        dzq[:, columns] = (d_act * slope[:, columns]).astype(BF)
        if columns is theirs:
            w.start(dzq.at[:, theirs], dzq2.at[1], s_dzq, p.partner, swaps)
    dzq2[0] = dzq[:, mine]
    sum2.relay()
    fold_r.step(3)
    twin_q.finish()
    w.arrive(dzq2.at[1], s_dzq, p.partner)
    for i, off in enumerate(ORDER):
        block = mod(z + off, SEQ)
        g_e[block] = dot_tn(q_ref[:, wide(block)], dzq2[...].reshape(2 * ROWS, 256)).astype(BF)
        if i == 0:
            fold_e.start()

    for index in (7, 8, 9, 10):
        loads[index].wait()
    share3, share4 = share_e(ew_ref, share1), share_r(rw_ref, share2)
    def optimizer(is_e, half, grad):
        refs = (
            (em_ref, e1_ref, e2_ref, eu_ref, em1_ref, ev_ref, w_e)
            if is_e
            else (rm_ref, r1_ref, r2_ref, ru_ref, rm1_ref, rv_ref, w_r)
        )
        at = pl.ds(pl.multiple_of(256 * half, 256), 256)
        at = (slice(None), at) if is_e else (at, slice(None))
        outs = adam_update(refs[0][at], refs[1][at], refs[2][at], grad)
        refs[3][at], refs[4][at], refs[5][at] = outs
        refs[6][at] = outs[0].astype(BF)

    def matrix(is_e, fold, swap, first):
        for s in range(first, 4):
            fold.step(s)
            yield
        total = fold.finish()
        for dd in range(2):
            at = slice(128 * dd, 128 * dd + 128)
            swap[dd] = (total[at] if is_e else total[:, at]).astype(BF)
        slot = w.slot()
        w.start(swap.at[1 - d], swap.at[2], slot, p.partner, swaps)
        optimizer(is_e, d, swap[d].astype(F32))
        yield
        w.arrive(swap.at[2], slot, p.partner)
        optimizer(is_e, 1 - d, swap[2].astype(F32))
        share = share3 if is_e else share4
        own = w_e if is_e else w_r

        def own_a(part):
            return own.at[span(0, part, 128), 0:256] if is_e else own.at[span(0, part, 192)]

        def own_b(part):
            return own.at[span(0, part, 128), 256:512] if is_e else own.at[span(192, part, 320)]

        share.start(own_a, own_b)
        keeps = []
        for src, dst in ((own_a, share.one_a), (own_b, share.one_b)):
            index = 11 + len(keeps) + 2 * is_e
            keeps.append(pltpu.make_async_copy(src(None), dst(z, d, None), local.at[index]))
            keeps[-1].start()
        yield
        share.open(own_b)
        for s in range(1, 5):
            yield
            share.ring_b.step(s)
            share.ring_a.step(s)
            share.ring_o.step(s)
        for keep in keeps:
            keep.wait()
        yield
        share.finish()

    def output():
        pl.when(p.low)(own_score)
        pl.when(jnp.logical_not(p.low))(lambda: clear(score2, r_rows))
        sum3 = Gather(w, p, parts3, near3, far3, False)
        sum3.compute_all(mixed_tile)
        yield
        sum3.relay()
        yield
        mixed_ref[...] = (block_of(q_ref, m)[0:ROWS].astype(F32) + sum3.finish()).astype(BF)

    def own_score():
        score2[...] = jnp.where(causal, sum2.finish(), 0.0).astype(BF)

    def mixed_tile(chip):
        first = dot(aq[...], rf[:, wide(chip)])
        return first - dot(score2[...], r_rows[:, :, wide(chip)].reshape(128, 256))

    take_turns(
        matrix(False, fold_r, swap_r, 4),
        matrix(True, fold_e, swap_e, 1),
        output(),
    )
    w.drain()


def clear(*refs):
    for ref in refs:
        ref[...] = jnp.zeros(ref.shape, ref.dtype)


def pass_on(*refs):
    *arrays, sems = refs
    count = len(arrays) // 3
    ins, outs = [], []
    for src, dst, held in zip(arrays[:count], arrays[count : 2 * count], arrays[2 * count :]):
        pieces = 8 if src.shape[0] * src.shape[1] > 100_000 else 1
        size = src.shape[0] // pieces
        for piece in range(pieces):
            rows = pl.ds(piece * size, size)
            index = len(ins)
            ins.append(pltpu.make_async_copy(src.at[rows], held.at[rows], sems.at[0, index]))
            outs.append(pltpu.make_async_copy(held.at[rows], dst.at[rows], sems.at[1, index]))
            ins[-1].start()
    for copy_in, copy_out in zip(ins, outs):
        copy_in.wait()
        copy_out.start()
    for copy_out in outs:
        copy_out.wait()


def body(
    query_rows, key_rows, value_rows, cotangent, inner_rate,
    expand_master, reduce_master, expand_first, reduce_first, expand_second, reduce_second,
):
    vmem = pl.BlockSpec(memory_space=pltpu.VMEM)
    hbm = pl.BlockSpec(memory_space=pl.ANY)
    e_shape, r_shape = expand_master.shape, reduce_master.shape

    def bf(*shape):
        return pltpu.VMEM(shape, BF)

    def f32(*shape):
        return pltpu.VMEM(shape, F32)

    outs = pl.pallas_call(
        kernel,
        out_shape=[
            jax.ShapeDtypeStruct((ROWS, 128), BF),
            jax.ShapeDtypeStruct(e_shape, F32),
            jax.ShapeDtypeStruct(r_shape, F32),
            jax.ShapeDtypeStruct(e_shape, F32),
            jax.ShapeDtypeStruct(r_shape, F32),
            jax.ShapeDtypeStruct(e_shape, F32),
            jax.ShapeDtypeStruct(r_shape, F32),
            jax.ShapeDtypeStruct((D, HID), BF),
            jax.ShapeDtypeStruct((HID, D), BF),
        ],
        in_specs=[hbm] * 11,
        out_specs=[vmem] * 7 + [hbm] * 2,
        scratch_shapes=[
            bf(2 * ROWS, D), bf(ROWS, D), bf(ROWS, D), bf(2 * ROWS, D), f32(1, ROWS),
            f32(*e_shape), f32(*r_shape), f32(*e_shape), f32(*r_shape), f32(*e_shape), f32(*r_shape),
            bf(D, HID), bf(HID, D),
            bf(SEQ, 16, D), bf(SEQ, 16, D),
            bf(12, SEQ, 16, HID), bf(12, SEQ, 16, HID),
            bf(ROWS, 1536), bf(ROWS, 1536),
            bf(ROWS, HID), f32(ROWS, HID),
            bf(ROWS, D), f32(ROWS, HID), f32(ROWS, HID),
            bf(2, 8, ROWS, 128), bf(8, ROWS, 128), bf(8, ROWS, 128),
            bf(2, 6, ROWS, 128), bf(6, ROWS, 128), bf(8, ROWS, 128),
            bf(2, 8, ROWS, 128), bf(8, ROWS, 128), bf(8, ROWS, 128),
            bf(ROWS, 128), bf(ROWS, HID), bf(ROWS, HID),
            bf(2, ROWS, 256), bf(2, ROWS, 256),
            bf(SEQ, 256, 256), bf(SEQ, 256, 256),
            bf(4, 128, 256), bf(4, 3, 256, 256),
            bf(3, 128, 256), bf(3, 256, 128),
            bf(128, HID), bf(HID, 128),
            pltpu.SemaphoreType.DMA((N_SEND,)),
            pltpu.SemaphoreType.DMA((N_RECV,)),
            pltpu.SemaphoreType.DMA((16,)),
        ],
        compiler_params=pltpu.CompilerParams(
            collective_id=0, has_side_effects=True, vmem_limit_bytes=56 * 1024 * 1024
        ),
        cost_estimate=pl.CostEstimate(
            flops=5_000_000_000, bytes_accessed=12_000_000, transcendentals=400_000
        ),
    )(
        query_rows[0], key_rows[0], value_rows[0], cotangent[0], inner_rate,
        expand_master, reduce_master, expand_first, reduce_first, expand_second, reduce_second,
    )
    outs = pl.pallas_call(
        pass_on,
        out_shape=[jax.ShapeDtypeStruct(out.shape, out.dtype) for out in outs],
        in_specs=[hbm] * 9,
        out_specs=[hbm] * 9,
        scratch_shapes=[pltpu.VMEM(out.shape, out.dtype) for out in outs]
        + [pltpu.SemaphoreType.DMA((2, 23))],
        compiler_params=pltpu.CompilerParams(vmem_limit_bytes=60 * 1024 * 1024),
        cost_estimate=pl.CostEstimate(flops=0, bytes_accessed=12_000_000, transcendentals=0),
    )(*outs)
    return (outs[0][None], *outs[1:])


def solution(mesh):
    in_specs = (
        P("dp", "seq", None),
        P("dp", "seq", None),
        P("dp", "seq", None),
        P("dp", "seq", None),
        P("dp", "seq"),
        P(("seq", "dp"), "mp"),
        P("mp", ("seq", "dp")),
        P(("seq", "dp"), "mp"),
        P("mp", ("seq", "dp")),
        P(("seq", "dp"), "mp"),
        P("mp", ("seq", "dp")),
    )
    out_specs = (
        P("dp", "seq", "mp"),
        P(("seq", "dp"), "mp"),
        P("mp", ("seq", "dp")),
        P(("seq", "dp"), "mp"),
        P("mp", ("seq", "dp")),
        P(("seq", "dp"), "mp"),
        P("mp", ("seq", "dp")),
        P(None, "mp"),
        P("mp", None),
    )
    return jax.shard_map(body, mesh=mesh, in_specs=in_specs, out_specs=out_specs, check_vma=False)
```
